256 devices in a mesh: batch: 32 (over x, z), node: 4 (over y), replica: 2 (over core).
Axes of the slice: x: 4, y: 4, z: 8, core: 2. Of those that a mesh axis runs over, the one named last changes fastest.
Arguments:
- embed_table: bfloat16 [32768, 1024], P('batch'), may hold values from -6 to 6
- owner_shard: int32 [64, 256, 1], P(('batch', 'replica')), may hold values from 0 to 31; in each aligned block of 256 rows (0 to 255, 256 to 511, ..., all dimensions but the last counted through in order) at most 12 rows name the same one
- local_row: int32 [64, 256], P(('batch', 'replica')), may hold values from 0 to 1023
- lengths: int32 [64], P(('batch', 'replica')), may hold values from 64 to 256
- spd_bucket: int32 [64, 256, 256], P(('batch', 'replica')), may hold values from 0 to 15, as said below
- degree_bucket: int32 [64, 256], P(('batch', 'replica')), may hold values from 0 to 31, as said below
- w_query: bfloat16 [1024, 1024], P(None, 'node'), may hold values from -0.1875 to 0.1875
- w_key: bfloat16 [1024, 1024], P(None, 'node'), may hold values from -0.1875 to 0.1875
- w_value: bfloat16 [1024, 1024], P(None, 'node'), may hold values from -0.1875 to 0.1875
- w_out: bfloat16 [1024, 1024], P('node'), may hold values from -0.1875 to 0.1875
- spd_bias: float32 [16, 16], P(None, 'node'), may hold values from -4 to 4
- degree_bias: float32 [32, 16], P(None, 'node'), may hold values from -2 to 253
- cotangent: bfloat16 [64, 256, 1024], P(('batch', 'replica')), may hold values from -6 to 6
Outputs:
- table_grad: float32 [32768, 1024], P('batch', ('node', 'replica'))
- query_grad: float32 [1024, 1024], P(None, 'node')
- key_grad: float32 [1024, 1024], P(None, 'node')
- value_grad: float32 [1024, 1024], P(None, 'node')
- out_grad: float32 [1024, 1024], P('node')
- spd_grad: float32 [16, 16], P(None, 'node')
- degree_grad: float32 [32, 16], P(None, 'node')
The draws below stay inside these ranges and needn't reach their ends.
Inputs may be any that keep to these rules, and one draw needn't show every extreme that they name: `owner_shard`: in each aligned block of 256 slots (the subgraphs of one index of batch and replica) no owner shard is named by more than 12 slots, a bound that some block reaches. `lengths`: slots at or past a subgraph's length are padding. `spd_bucket`: symmetric in its last two dimensions, 0 exactly on the diagonal. `degree_bucket`: some subgraphs hold only buckets below half of 32.
All inputs are finite; a program needn't handle non-finite values.
Results may differ from the reference program's by a relative error of at most 0.015.
Values may be sent and summed in bfloat16 or wider, within the bound.
A program may use at most 64 MiB of HBM per device.

```python
import math
import jax
import jax.numpy as jnp
import numpy as np
from jax import lax

D = 1024
HEADS = 16
HEAD_DIM = 64
S = 256
NSPD = 16
NDEG = 32
G_DEV = 1
ROWS_DEV = 1024
NODES = 32768
NSUB = 64
CAP = 12
N_BATCH = 32
N_REPLICA = 2


def draw_spd_bucket(key, part):
    upper = jax.random.randint(key, (NSUB, S, S), 1, NSPD)
    row_pos = jnp.arange(S)[:, None]
    col_pos = jnp.arange(S)[None, :]
    mirrored = jnp.where(row_pos < col_pos, upper, jnp.swapaxes(upper, 1, 2))
    return jnp.where(row_pos == col_pos, 0, mirrored).astype(jnp.int32)


def draw_degree_bucket(key, part):
    hub_flag = jax.random.randint(jax.random.fold_in(key, 1), (NSUB, 1), 0, 2)
    lower_half = jax.random.randint(jax.random.fold_in(key, 2), (NSUB, S), 0, NDEG // 2)
    full_range = jax.random.randint(jax.random.fold_in(key, 3), (NSUB, S), 0, NDEG)
    return jnp.where(hub_flag == 1, full_range, lower_half).astype(jnp.int32)


def draw_degree_bias(key, part):
    base = jax.random.uniform(jax.random.fold_in(key, 4), (NDEG, HEADS), jnp.float32, -2.0, 2.0)
    return base.astype(jnp.float32)


def touch_ends(values, rng, low, largest):
    index_at = [jax.random.randint(jax.random.fold_in(rng, axis), (), 0, length) for axis, length in enumerate(values.shape)]
    main_axis = values.shape.index(max(values.shape))
    beside = index_at[:main_axis] + [(index_at[main_axis] + 1) % values.shape[main_axis]] + index_at[main_axis + 1:]
    return values.at[tuple(index_at)].set(low).at[tuple(beside)].set(largest)


def level_of(own_key, dims, split, least, largest):
    def one(position, shards_of):
        heights = jax.random.uniform(jax.random.fold_in(jax.random.fold_in(own_key, 6), position), (shards_of,), jnp.float32, least / len(split), largest / len(split))
        return jnp.repeat(jnp.exp(heights), dims[position] // shards_of).reshape((-1,) + (1,) * (len(dims) - position - 1))

    level = one(*split[0])
    for cut in split[1:]:
        level = level * one(*cut)
    return level


def rank_bounds(amount, lean):
    loads = [(1 << 20) // math.isqrt(standing ** lean) + 1 for standing in range(1, amount + 1)]
    width = 1 + sum(loads) // (1 << 30)
    return np.cumsum(np.array([max(1, weight // width) for weight in loads]))


def ranked_ids(own_key, shape, count, skew):
    grid = rank_bounds(count, skew)
    lot = jax.random.randint(jax.random.fold_in(own_key, 1), shape, 0, int(grid[count - 1]))
    grade = jnp.searchsorted(jnp.asarray(grid, jnp.int32), lot, side="right")
    return jax.random.permutation(jax.random.fold_in(own_key, 2), count)[grade].astype(jnp.int32)


def assign_block(rng, own, number, rows, amount, top, reach, slope):
    sequence = jax.random.permutation(rng, amount)
    packed, common = portions_of(amount, rows * top, reach, slope, True), portions_of(amount, rows * top, reach, slope, False)
    places = jnp.arange(amount)

    def named(tallies, turn):
        used = int((tallies > 0).sum())
        fixed = max(1, used // 4)
        shifted = fixed + (places - fixed + turn * (used - fixed)) % max(1, amount - fixed)
        return jnp.zeros((amount,), jnp.int32).at[sequence[jnp.where(places < fixed, places, shifted)]].set(jnp.asarray(tallies, jnp.int32))

    tallies = jnp.where(number % 4 == 0, named(packed, number // 4), named(common, number - number // 4 - 1))
    mixed = jax.random.permutation(jax.random.fold_in(own, 3), amount)
    source_of, sink = mixed[0:amount // 2 * 2:2], mixed[1:amount // 2 * 2:2]
    margin = jnp.minimum(tallies[source_of] - 1, reach - tallies[sink]) // 2
    margin = jnp.where((source_of == sequence[0]) | (sink == sequence[0]) | (tallies[sink] == 0), 0, jnp.maximum(margin, 0))
    shifted = jax.random.randint(jax.random.fold_in(own, 4), (amount // 2,), 0, 1 << 20) % (margin + 1)
    tallies = tallies.at[source_of].add(-shifted).at[sink].add(shifted)
    members = jnp.searchsorted(jnp.cumsum(tallies), jnp.arange(rows * top), side="right").astype(jnp.int32)
    listing = members.reshape(top, rows).T
    listing = listing[jax.random.permutation(jax.random.fold_in(own, 1), rows)]
    turn = jax.random.randint(jax.random.fold_in(own, 2), (rows, 1), 0, top)
    return jnp.take_along_axis(listing, (jnp.arange(top)[None, :] + turn) % top, axis=1)


def portions_of(number_of, total, reach, slope, full):
    weights = [(1 << 20) // math.isqrt(standing ** slope) + 1 for standing in range(1, number_of + 1)]
    largest = reach if full else min(reach, max(-(-total // number_of), total * weights[0] // sum(weights)))
    least = 1 if total - largest >= number_of - 1 else 0
    holding, spare = [largest] + [least] * (number_of - 1), total - largest - least * (number_of - 1)
    while spare > 0:
        candidates = [i for i in range(1, number_of) if holding[i] < largest] or [i for i in range(1, number_of) if holding[i] < reach]
        mass, remaining = sum([weights[i] for i in candidates]), spare
        for i in candidates:
            more = min(reach - holding[i], max(1, remaining * weights[i] // mass), spare)
            holding[i] = holding[i] + more
            spare = spare - more
    return np.array(holding)


def scatter_about(rng, dims, deviation, limit, cuts=(), kind=jnp.bfloat16):
    result = deviation * jax.random.normal(rng, dims, jnp.float32)
    if cuts:
        result = result * level_of(rng, dims, cuts, -0.22, 0.18)
    return jnp.clip(result, -limit, limit).astype(kind)


def setup_inputs(seed: int = 0) -> dict:
    key_list = jax.random.split(jax.random.key(seed), 14)
    embed_table = scatter_about(key_list[0], (NODES, D), 1.0, 6.0, ((0, 32),))
    owner_shard_keys = jax.random.split(jax.random.fold_in(key_list[1], 1), NSUB * S // (G_DEV * S))
    owner_shard_turns = jax.random.permutation(jax.random.fold_in(key_list[1], 3), NSUB * S // (G_DEV * S))
    owner_shard = jax.vmap(lambda own, number: assign_block(jax.random.fold_in(key_list[1], 2), own, number, G_DEV * S, N_BATCH, 1, CAP, 2))(owner_shard_keys, owner_shard_turns).reshape((NSUB, S, 1))
    local_row = touch_ends(ranked_ids(key_list[2], (NSUB, S), ROWS_DEV, 2), jax.random.fold_in(key_list[2], 3), 0, ROWS_DEV - 1).astype(jnp.int32)
    lengths = touch_ends(jax.random.randint(key_list[3], (NSUB,), S // 4, S + 1), jax.random.fold_in(key_list[3], 1), S // 4, S).astype(jnp.int32)
    spd_bucket = draw_spd_bucket(jax.random.fold_in(key_list[13], 71), 0)
    degree_bucket = draw_degree_bucket(jax.random.fold_in(key_list[13], 71), 0)
    w_query = scatter_about(key_list[6], (D, D), D ** -0.5, 0.1875, ((1, 4),))
    w_key = scatter_about(key_list[7], (D, D), D ** -0.5, 0.1875, ((1, 4),))
    w_value = scatter_about(key_list[8], (D, D), D ** -0.5, 0.1875, ((1, 4),))
    w_out = scatter_about(key_list[9], (D, D), D ** -0.5, 0.1875, ((0, 4),))
    spd_bias = scatter_about(key_list[10], (NSPD, HEADS), 1.0, 4.0, ((1, 4),), jnp.float32)
    degree_bias = draw_degree_bias(jax.random.fold_in(key_list[13], 71), 0)
    cotangent = scatter_about(key_list[12], (NSUB, S, D), 1.0, 6.0, ((0, 64),))
    return {"embed_table": embed_table, "owner_shard": owner_shard, "local_row": local_row, "lengths": lengths, "spd_bucket": spd_bucket, "degree_bucket": degree_bucket, "w_query": w_query, "w_key": w_key, "w_value": w_value, "w_out": w_out, "spd_bias": spd_bias, "degree_bias": degree_bias, "cotangent": cotangent}


EPS = 1e-05

def normalize(rows_in):
    widened = rows_in.astype(jnp.float32)
    mean_val = lax.optimization_barrier(jnp.mean(widened, axis=-1, keepdims=True))
    centred = widened - mean_val
    inv_std = lax.rsqrt(lax.optimization_barrier(jnp.mean(centred * centred, axis=-1, keepdims=True)) + EPS)
    return (centred * inv_std, inv_std)

def reference(embed_table, owner_shard, local_row, lengths, spd_bucket, degree_bucket, w_query, w_key, w_value, w_out, spd_bias, degree_bias, cotangent):
    node_ids = owner_shard[:, :, 0] * ROWS_DEV + local_row
    group_total = NSUB // G_DEV

    def by_group(array_in):
        return array_in.reshape((group_total, G_DEV) + array_in.shape[1:])
    scanned = (by_group(node_ids), by_group(lengths), by_group(spd_bucket), by_group(degree_bucket), by_group(cotangent))
    score_scale = HEAD_DIM ** (-0.5)
    head_shape = (G_DEV, S, HEADS, HEAD_DIM)
    initial = (jnp.zeros((NODES, D), jnp.float32), jnp.zeros((D, D), jnp.float32), jnp.zeros((D, D), jnp.float32), jnp.zeros((D, D), jnp.float32), jnp.zeros((D, D), jnp.float32), jnp.zeros((NSPD, HEADS), jnp.float32), jnp.zeros((NDEG, HEADS), jnp.float32))

    def layer_step(carry, inputs):
        table_acc, query_acc, key_acc, value_acc, out_acc, spd_acc, degree_acc = carry
        node_blk, length_blk, spd_blk, degree_blk, cot_blk = inputs
        flat_nodes = node_blk.reshape(G_DEV * S).astype(jnp.int32)
        slot_rows = embed_table[flat_nodes]
        x_hat, inv_std = normalize(slot_rows)
        normed = x_hat.astype(jnp.bfloat16)

        def project(weight):
            return jnp.dot(normed, weight, preferred_element_type=jnp.float32).astype(jnp.bfloat16)
        queries = project(w_query)
        key_rows = project(w_key)
        values = project(w_value)
        queries_h = queries.reshape(head_shape).astype(jnp.float32)
        keys_h = key_rows.reshape(head_shape).astype(jnp.float32)
        values_h = values.reshape(head_shape).astype(jnp.float32)
        valid_slot = jnp.arange(S, dtype=jnp.int32)[None, :] < length_blk[:, None]
        spd_term = jnp.transpose(spd_bias[spd_blk], (0, 3, 1, 2))
        degree_term = jnp.transpose(degree_bias[degree_blk], (0, 2, 1))[:, :, None, :]
        scores = jnp.einsum('gihd,gjhd->ghij', queries_h, keys_h) * score_scale + spd_term + degree_term
        scores = jnp.where(valid_slot[:, None, None, :], scores, -jnp.inf)
        row_top = lax.optimization_barrier(jnp.max(scores, axis=-1, keepdims=True))
        exp_scores = jnp.exp(scores - row_top)
        probs = exp_scores / lax.optimization_barrier(jnp.sum(exp_scores, axis=-1, keepdims=True))
        probs_b = probs.astype(jnp.bfloat16)
        attended = jnp.einsum('ghij,gjhd->gihd', probs_b.astype(jnp.float32), values_h).astype(jnp.bfloat16).reshape(G_DEV * S, D)
        d_masked = jnp.where(valid_slot[:, :, None], cot_blk, jnp.zeros_like(cot_blk)).reshape(G_DEV * S, D)
        d_att = jnp.dot(d_masked, w_out.T, preferred_element_type=jnp.float32).astype(jnp.bfloat16)
        out_acc = out_acc + jnp.dot(attended.T, d_masked, preferred_element_type=jnp.float32)
        d_att_h = d_att.reshape(head_shape).astype(jnp.float32)
        d_values = jnp.einsum('ghij,gihd->gjhd', probs_b.astype(jnp.float32), d_att_h).astype(jnp.bfloat16).reshape(G_DEV * S, D)
        d_probs = jnp.einsum('gihd,gjhd->ghij', d_att_h, values_h)
        d_scores = probs * (d_probs - lax.optimization_barrier(jnp.sum(probs * d_probs, axis=-1, keepdims=True)))
        spd_acc = spd_acc.at[spd_blk].add(jnp.transpose(d_scores, (0, 2, 3, 1)))
        degree_acc = degree_acc.at[degree_blk].add(jnp.transpose(lax.optimization_barrier(jnp.sum(d_scores, axis=2)), (0, 2, 1)))
        d_scores_b = d_scores.astype(jnp.bfloat16).astype(jnp.float32)
        d_queries = (jnp.einsum('ghij,gjhd->gihd', d_scores_b, keys_h) * score_scale).astype(jnp.bfloat16).reshape(G_DEV * S, D)
        d_keys = (jnp.einsum('ghij,gihd->gjhd', d_scores_b, queries_h) * score_scale).astype(jnp.bfloat16).reshape(G_DEV * S, D)
        query_acc = query_acc + jnp.dot(normed.T, d_queries, preferred_element_type=jnp.float32)
        key_acc = key_acc + jnp.dot(normed.T, d_keys, preferred_element_type=jnp.float32)
        value_acc = value_acc + jnp.dot(normed.T, d_values, preferred_element_type=jnp.float32)
        d_normed = jnp.dot(d_queries, w_query.T, preferred_element_type=jnp.float32) + jnp.dot(d_keys, w_key.T, preferred_element_type=jnp.float32) + jnp.dot(d_values, w_value.T, preferred_element_type=jnp.float32)
        d_rows = d_masked.astype(jnp.float32) + inv_std * (d_normed - lax.optimization_barrier(jnp.mean(d_normed, axis=-1, keepdims=True)) - x_hat * lax.optimization_barrier(jnp.mean(d_normed * x_hat, axis=-1, keepdims=True)))
        table_acc = table_acc.at[flat_nodes].add(d_rows)
        return ((table_acc, query_acc, key_acc, value_acc, out_acc, spd_acc, degree_acc), None)
    final, _ = lax.scan(layer_step, initial, scanned)
    copies = float(N_BATCH * N_REPLICA)
    return (final[0], final[1] / copies, final[2] / copies, final[3] / copies, final[4] / copies, final[5] / copies, final[6] / copies)
```

```python
import functools

import jax
import jax.numpy as jnp
from jax import lax
from jax.experimental import pallas as pl
from jax.experimental.pallas import tpu as pltpu
from jax.sharding import PartitionSpec as P

HEAD_DIM = 64
NSPD = 16
NDEG = 32
EPS = 1e-05
PAIR_ROWS = 16
Z_SIZE = 8
MESH = pl.DeviceIdType.MESH
F32 = jnp.float32
BF16 = jnp.bfloat16
I32 = jnp.int32


def iota(shape, dim):
    return lax.broadcasted_iota(I32, shape, dim)


def dot(a, b, ca=1, cb=0, precision=None):
    return lax.dot_general(
        a, b, (((ca,), (cb,)), ((), ())), preferred_element_type=F32, precision=precision
    )


def remote(src, dst, send_sem, recv_sem, **where):
    return pltpu.make_async_remote_copy(
        src_ref=src,
        dst_ref=dst,
        send_sem=send_sem,
        recv_sem=recv_sem,
        device_id=where,
        device_id_type=MESH,
    )


def wait_bytes(ref, sem):
    pltpu.make_async_copy(ref, ref, sem).wait()


def greet(batch, nodes, n_batch, n_node):
    me_b, me_n, me_r = lax.axis_index("batch"), lax.axis_index("node"), lax.axis_index("replica")
    barrier = pltpu.get_barrier_semaphore()

    if batch:

        def body(j, carry):
            pl.semaphore_signal(
                barrier, inc=1, device_id={"batch": lax.rem(me_b + j, n_batch)}, device_id_type=MESH
            )
            return carry

        lax.fori_loop(1, n_batch, body, 0)
    if nodes:
        for j in range(1, n_node):
            pl.semaphore_signal(
                barrier, inc=1, device_id={"node": lax.rem(me_n + j, n_node)}, device_id_type=MESH
            )
    pl.semaphore_signal(barrier, inc=1, device_id={"replica": 1 - me_r}, device_id_type=MESH)
    pl.semaphore_wait(barrier, (n_batch - 1) * batch + (n_node - 1) * nodes + 1)


def fetch_kernel(
    n_batch,
    n_node,
    owner_ref,
    local_ref,
    table_ref,
    rows_ref,
    reqs_ref,
    dest_ref,
    table_v,
    ask,
    spread,
    rows_send,
    rows_recv,
    local_sem,
    ssem,
    rsem,
):
    me_b, me_n, me_r = lax.axis_index("batch"), lax.axis_index("node"), lax.axis_index("replica")
    slots = owner_ref.shape[1]
    width = table_v.shape[1]
    table_rows = table_v.shape[0]
    entries = n_batch * PAIR_ROWS
    load = pltpu.make_async_copy(
        table_ref.at[:, pl.ds(pl.multiple_of(me_n * width, width), width)], table_v, local_sem
    )
    load.start()

    owner_row = owner_ref[...]
    across = jnp.broadcast_to(owner_row, (slots, slots))
    down = jnp.transpose(across)
    same = across == down
    r0, r1 = iota((slots, slots), 0), iota((slots, slots), 1)
    rank_row = jnp.sum(jnp.where(same & (r0 < r1), 1.0, 0.0), axis=0, keepdims=True).astype(I32)
    rank_col = jnp.sum(jnp.where(same & (r1 < r0), 1.0, 0.0), axis=1, keepdims=True).astype(I32)
    dest_ref[...] = owner_row * PAIR_ROWS + rank_row
    dest_col = down[:, 0:1] * PAIR_ROWS + rank_col

    wanted = local_ref[...] + 1
    hit = owner_row == iota((n_batch, slots), 0)
    high = jnp.where(hit, (wanted // 32).astype(F32), 0.0).astype(BF16)
    low = jnp.where(hit, (wanted % 32).astype(F32), 0.0).astype(BF16)
    at_rank = jnp.where(rank_col == iota((slots, 128), 1), 1.0, 0.0).astype(BF16)
    listed = (dot(high, at_rank) * 32.0 + dot(low, at_rank)).astype(I32)
    for o in range(n_batch):
        ask[o] = listed[o : o + 1, :]

    greet(True, True, n_batch, n_node)

    def send_ask(j, carry):
        p = lax.rem(me_b + j, n_batch)
        remote(ask.at[p], reqs_ref.at[me_r, me_b], ssem.at[0], rsem.at[0], batch=p).start()
        return carry

    lax.fori_loop(1, n_batch, send_ask, 0)
    reqs_ref[me_r, me_b] = ask[me_b]
    load.wait()
    wait_bytes(ask.at[pl.ds(0, n_batch - 1)], rsem.at[0])
    remote(
        reqs_ref.at[me_r], reqs_ref.at[me_r], ssem.at[1], rsem.at[1], replica=1 - me_r
    ).start()

    for p in range(n_batch):
        spread[p * PAIR_ROWS : (p + 1) * PAIR_ROWS, :] = jnp.broadcast_to(
            reqs_ref[me_r, p], (PAIR_ROWS, 128)
        )
    mine = iota((entries, 128), 1) == iota((entries, 128), 0) % PAIR_ROWS
    target = (
        jnp.sum(jnp.where(mine, spread[...].astype(F32), 0.0), axis=1, keepdims=True).astype(I32) - 1
    )
    pick = jnp.where(iota((entries, table_rows), 1) == target, 1.0, 0.0).astype(BF16)
    rows_send[...] = (
        dot(pick, table_v[...]).astype(BF16).reshape(n_batch, PAIR_ROWS, width)
    )

    def send_rows(j, carry):
        p = lax.rem(me_b + j, n_batch)
        remote(rows_send.at[p], rows_recv.at[me_b], ssem.at[2], rsem.at[2], batch=p).start()
        return carry

    lax.fori_loop(1, n_batch, send_rows, 0)
    rows_recv[me_b] = rows_send[me_b]
    place = jnp.where(iota((slots, entries), 1) == dest_col, 1.0, 0.0).astype(BF16)
    wait_bytes(rows_recv.at[pl.ds(0, n_batch - 1)], rsem.at[2])
    rows_ref[me_n] = dot(place, rows_recv[...].reshape(entries, width)).astype(BF16)
    for j in range(1, n_node):
        remote(
            rows_ref.at[me_n],
            rows_ref.at[me_n],
            ssem.at[3],
            rsem.at[3],
            node=lax.rem(me_n + j, n_node),
        ).start()
    wait_bytes(rows_ref.at[pl.ds(0, n_node - 1)], rsem.at[3])
    wait_bytes(reqs_ref.at[0], rsem.at[1])
    wait_bytes(ask.at[pl.ds(0, n_batch - 1)], ssem.at[0])
    wait_bytes(reqs_ref.at[0], ssem.at[1])
    wait_bytes(rows_send.at[pl.ds(0, n_batch - 1)], ssem.at[2])
    wait_bytes(rows_ref.at[pl.ds(0, n_node - 1)], ssem.at[3])


def layer_kernel(
    length_ref,
    spd_bias_ref,
    deg_bias_ref,
    rows_ref,
    spd_ref,
    deg_ref,
    cot_ref,
    wq_ref,
    wk_ref,
    wv_ref,
    wo_ref,
    grads_ref,
    d_rows_ref,
    small_ref,
    bias,
    d_scores,
    sums,
):
    slots, feature_dim = cot_ref.shape
    width = wq_ref.shape[1]
    heads = width // HEAD_DIM
    blocks = feature_dim // width
    length = length_ref[0]
    scale = HEAD_DIM ** (-0.5)
    step = 32

    def bias_block(i, carry):
        rows = pl.ds(pl.multiple_of(i * step, step), step)
        bucket = spd_ref[rows, :]
        terms = [jnp.full(bucket.shape, spd_bias_ref[0, h], F32) for h in range(heads)]
        for b in range(1, NSPD):
            is_b = bucket == b
            terms = [jnp.where(is_b, spd_bias_ref[b, h], terms[h]) for h in range(heads)]
        for h in range(heads):
            bias[h, rows, :] = terms[h]
        return carry

    lax.fori_loop(0, slots // step, bias_block, 0)
    degree = deg_ref[...]
    deg_terms = []
    for h in range(heads):
        term = jnp.full(degree.shape, deg_bias_ref[0, h], F32)
        for b in range(1, NDEG):
            term = jnp.where(degree == b, deg_bias_ref[b, h], term)
        deg_terms.append(term)

    cot = cot_ref[...]
    d_masked = jnp.where(iota((slots, feature_dim), 0) < length, cot.astype(F32), 0.0).astype(BF16)
    d_att = dot(d_masked, wo_ref[...], 1, 1).astype(BF16)

    x = jnp.concatenate([rows_ref[b] for b in range(blocks)], axis=1).astype(F32)
    centred = x - jnp.mean(x, axis=1, keepdims=True)
    inv_std = lax.rsqrt(jnp.mean(centred * centred, axis=1, keepdims=True) + EPS)
    x_hat = centred * inv_std
    normed = x_hat.astype(BF16)
    queries = dot(normed, wq_ref[...]).astype(BF16)
    keys = dot(normed, wk_ref[...]).astype(BF16)
    values = dot(normed, wv_ref[...]).astype(BF16)

    lane_head = iota((slots, width), 1) // HEAD_DIM

    def only(h, a):
        return jnp.where(lane_head == h, a, jnp.zeros_like(a))

    valid = iota((slots, slots), 1) < length
    attended = jnp.zeros((slots, width), F32)
    d_values = jnp.zeros((slots, width), F32)
    d_queries = jnp.zeros((slots, width), F32)
    d_keys = jnp.zeros((slots, width), F32)
    for h in range(heads):
        q_h, k_h, v_h, da_h = only(h, queries), only(h, keys), only(h, values), only(h, d_att)
        scores = dot(q_h, keys, 1, 1) * scale + bias[h] + deg_terms[h]
        scores = jnp.where(valid, scores, -jnp.inf)
        exps = jnp.exp(scores - jnp.max(scores, axis=1, keepdims=True))
        probs = exps / jnp.sum(exps, axis=1, keepdims=True)
        probs_b = probs.astype(BF16)
        attended = attended + dot(probs_b, v_h)
        d_values = d_values + dot(probs_b, da_h, 0, 0)
        d_probs = dot(da_h, values, 1, 1)
        ds = probs * (d_probs - jnp.sum(probs * d_probs, axis=1, keepdims=True))
        d_scores[h] = ds
        ds_b = ds.astype(BF16)
        d_queries = d_queries + dot(ds_b, k_h)
        d_keys = d_keys + dot(ds_b, q_h, 0, 0)
    attended = attended.astype(BF16)
    d_queries = (d_queries * scale).astype(BF16)
    d_keys = (d_keys * scale).astype(BF16)
    d_values = d_values.astype(BF16)

    halves = (2, 4, feature_dim // 8, width)
    out_part = dot(attended, d_masked, 0, 0).astype(BF16)
    for b in range(blocks):
        for k in range(2):
            grads_ref[0, b // 2, 2 * (b % 2) + k] = out_part[
                k * 128 : (k + 1) * 128, b * width : (b + 1) * width
            ]
    normed_t = jnp.transpose(normed)
    grads_ref[1] = dot(normed_t, d_values).astype(BF16).reshape(halves)
    grads_ref[2] = dot(normed_t, d_keys).astype(BF16).reshape(halves)
    grads_ref[3] = dot(normed_t, d_queries).astype(BF16).reshape(halves)

    d_normed = (
        dot(d_queries, wq_ref[...], 1, 1)
        + dot(d_keys, wk_ref[...], 1, 1)
        + dot(d_values, wv_ref[...], 1, 1)
    )
    lead = jnp.where(lax.axis_index("node") == 0, 1.0, 0.0)
    d_rows = lead * d_masked.astype(F32) + inv_std * (
        d_normed
        - jnp.mean(d_normed, axis=1, keepdims=True)
        - x_hat * jnp.mean(d_normed * x_hat, axis=1, keepdims=True)
    )
    for b in range(blocks):
        d_rows_ref[b] = d_rows[:, b * width : (b + 1) * width].astype(BF16)

    per_head = NSPD + NDEG
    sums[...] = jnp.zeros_like(sums)
    for h in range(heads):

        def spd_block(i, totals):
            rows = pl.ds(pl.multiple_of(i * step, step), step)
            bucket, ds = spd_ref[rows, :], d_scores[h, rows, :]
            new = []
            for b in range(NSPD):
                kept = jnp.where(bucket == b, ds, 0.0)
                kept = kept[:, :128] + kept[:, 128:]
                new.append(
                    totals[b] + (kept[0:8] + kept[8:16]) + (kept[16:24] + kept[24:32])
                )
            return tuple(new)

        totals = lax.fori_loop(
            0, slots // step, spd_block, tuple(jnp.zeros((8, 128), F32) for _ in range(NSPD))
        )
        for b in range(NSPD):
            at = h * per_head + b
            sums[at : at + 1, :] = jnp.sum(totals[b], axis=0, keepdims=True)
        by_key = jnp.sum(d_scores[h], axis=0, keepdims=True)
        kept = jnp.where(degree == iota((NDEG, slots), 0), by_key, 0.0)
        at = h * per_head + NSPD
        sums[at : at + NDEG, :] = kept[:, :128] + kept[:, 128:]
    small_ref[...] = dot(
        jnp.ones((8, 128), F32), sums[...], 1, 1, precision=lax.Precision.HIGHEST
    )


def reduce_kernel(
    n_batch,
    n_node,
    grads_ref,
    d_rows_ref,
    small_ref,
    dest_ref,
    reqs_ref,
    out_ref,
    table_ref,
    small_out,
    core_in,
    core_sum,
    x_in,
    x_sum,
    z_in,
    y_in,
    pack,
    to_core,
    table_in,
    small_core,
    small_x,
    small_z,
    spread,
    ssem,
    rsem,
    fs,
    fr,
    ts,
    tr,
):
    me_b, me_n, me_r = lax.axis_index("batch"), lax.axis_index("node"), lax.axis_index("replica")
    n_z = Z_SIZE
    n_x = n_batch // n_z
    me_x, me_z = me_b // n_z, me_b % n_z
    other = 1 - me_r
    chunks = grads_ref.shape[0]
    slots = dest_ref.shape[1]
    width = d_rows_ref.shape[2]
    half = width // 2
    entries = n_batch * PAIR_ROWS
    copies = 2.0 * n_batch
    piece = x_sum.shape[2]

    greet(True, True, n_batch, n_node)

    for j in range(1, n_node):
        p = lax.rem(me_n + j, n_node)
        remote(d_rows_ref.at[p], y_in.at[me_n], fs.at[0], fr.at[0], node=p).start()
    for c in range(chunks):
        remote(
            grads_ref.at[c, other], core_in.at[c], ssem.at[0, c], rsem.at[0, c], replica=other
        ).start()
    remote(small_ref, small_core, ts.at[0], tr.at[0], replica=other).start()
    y_in[me_n] = d_rows_ref[me_n]

    for c in range(chunks):
        wait_bytes(core_in.at[c], rsem.at[0, c])
        core_sum[c] = (grads_ref[c, me_r].astype(F32) + core_in[c].astype(F32)).astype(BF16)
        for j in range(1, n_x):
            p = lax.rem(me_x + j, n_x)
            remote(
                core_sum.at[c, p],
                x_in.at[c, me_x],
                ssem.at[1, c],
                rsem.at[1, c],
                batch=p * n_z + me_z,
            ).start()
        x_in[c, me_x] = core_sum[c, me_x]

    wait_bytes(small_core, tr.at[0])
    small_x[me_x] = small_ref[...] + small_core[...]
    for j in range(1, n_x):
        p = lax.rem(me_x + j, n_x)
        remote(
            small_x.at[me_x], small_x.at[me_x], ts.at[1], tr.at[1], batch=p * n_z + me_z
        ).start()

    place = jnp.where(iota((entries, slots), 0) == dest_ref[...], 1.0, 0.0).astype(BF16)
    wait_bytes(y_in.at[pl.ds(0, n_node - 1)], fr.at[0])
    d_rows = y_in[0].astype(F32)
    for n in range(1, n_node):
        d_rows = d_rows + y_in[n].astype(F32)
    packed = dot(place, d_rows.astype(BF16)).astype(BF16)
    left, right = packed[:, :half], packed[:, half:]
    shape = (n_batch, PAIR_ROWS, half)
    pack[me_r] = jnp.where(me_r == 0, left, right).reshape(shape)
    to_core[...] = jnp.where(me_r == 0, right, left).reshape(shape)
    remote(to_core, pack.at[me_r], fs.at[1], fr.at[1], replica=other).start()

    for c in range(chunks):
        wait_bytes(x_in.at[c, pl.ds(0, n_x - 1)], rsem.at[1, c])
        total = x_in[c, 0].astype(F32)
        for x in range(1, n_x):
            total = total + x_in[c, x].astype(F32)
        x_sum[c] = total.astype(BF16).reshape(n_z, piece, width)
        for j in range(1, n_z):
            p = lax.rem(me_z + j, n_z)
            remote(
                x_sum.at[c, p],
                z_in.at[c, me_z],
                ssem.at[2, c],
                rsem.at[2, c],
                batch=me_x * n_z + p,
            ).start()
        z_in[c, me_z] = x_sum[c, me_z]

    wait_bytes(small_x.at[pl.ds(0, n_x - 1)], tr.at[1])
    total = small_x[0]
    for x in range(1, n_x):
        total = total + small_x[x]
    small_z[me_z] = total
    for j in range(1, n_z):
        p = lax.rem(me_z + j, n_z)
        remote(
            small_z.at[me_z], small_z.at[me_z], ts.at[2], tr.at[2], batch=me_x * n_z + p
        ).start()

    wait_bytes(to_core, fr.at[1])

    def send_pack(j, carry):
        p = lax.rem(me_b + j, n_batch)
        remote(pack.at[:, p], table_in.at[:, me_b], fs.at[2], fr.at[2], batch=p).start()
        return carry

    lax.fori_loop(1, n_batch, send_pack, 0)
    table_in[:, me_b] = pack[:, me_b]

    for c in range(chunks):
        wait_bytes(z_in.at[c, pl.ds(0, n_z - 1)], rsem.at[2, c])
        total = z_in[c, 0].astype(F32)
        for z in range(1, n_z):
            total = total + z_in[c, z].astype(F32)
        out_ref[c, me_r, me_x, me_z] = (total * (1.0 / copies)).astype(BF16)
        for j in range(1, n_z):
            p = lax.rem(me_z + j, n_z)
            mine = out_ref.at[c, me_r, me_x, me_z]
            remote(mine, mine, ssem.at[3, c], rsem.at[3, c], batch=me_x * n_z + p).start()

    mine = iota((entries, 128), 1) == iota((entries, 128), 0) % PAIR_ROWS
    targets = []
    for r in range(2):
        for p in range(n_batch):
            spread[p * PAIR_ROWS : (p + 1) * PAIR_ROWS, :] = jnp.broadcast_to(
                reqs_ref[r, p], (PAIR_ROWS, 128)
            )
        target = jnp.sum(jnp.where(mine, spread[...].astype(F32), 0.0), axis=1, keepdims=True) - 1.0
        flat = jnp.transpose(jnp.broadcast_to(target, (entries, 128)))[0:1, :].astype(I32)
        targets.append(flat)

    for c in range(chunks):
        wait_bytes(out_ref.at[c, 0, 0, pl.ds(0, n_z - 1)], rsem.at[3, c])
        for j in range(1, n_x):
            p = lax.rem(me_x + j, n_x)
            mine = out_ref.at[c, me_r, me_x]
            remote(mine, mine, ssem.at[4, c], rsem.at[4, c], batch=p * n_z + me_z).start()

    wait_bytes(small_z.at[pl.ds(0, n_z - 1)], tr.at[2])
    total = small_z[0]
    for z in range(1, n_z):
        total = total + small_z[z]
    small_out[...] = total * (1.0 / copies)

    table_rows = table_ref.shape[0]
    row = iota((table_rows, entries), 0)
    scatter = [jnp.where(row == t, 1.0, 0.0).astype(BF16) for t in targets]
    wait_bytes(table_in.at[:, pl.ds(0, n_batch - 1)], fr.at[2])
    table_ref[...] = dot(scatter[0], table_in[0].reshape(entries, half)) + dot(
        scatter[1], table_in[1].reshape(entries, half)
    )

    for c in range(chunks):
        wait_bytes(out_ref.at[c, 0, pl.ds(0, n_x - 1)], rsem.at[4, c])
        mine = out_ref.at[c, me_r]
        remote(mine, mine, ssem.at[5, c], rsem.at[5, c], replica=other).start()
    for c in range(chunks):
        wait_bytes(out_ref.at[c, 0], rsem.at[5, c])

    wait_bytes(y_in.at[pl.ds(0, n_node - 1)], fs.at[0])
    wait_bytes(to_core, fs.at[1])
    wait_bytes(table_in.at[:, pl.ds(0, n_batch - 1)], fs.at[2])
    wait_bytes(small_core, ts.at[0])
    wait_bytes(small_x.at[pl.ds(0, n_x - 1)], ts.at[1])
    wait_bytes(small_z.at[pl.ds(0, n_z - 1)], ts.at[2])
    for c in range(chunks):
        wait_bytes(core_in.at[c], ssem.at[0, c])
        wait_bytes(x_in.at[c, pl.ds(0, n_x - 1)], ssem.at[1, c])
        wait_bytes(z_in.at[c, pl.ds(0, n_z - 1)], ssem.at[2, c])
        wait_bytes(out_ref.at[c, 0, 0, pl.ds(0, n_z - 1)], ssem.at[3, c])
        wait_bytes(out_ref.at[c, 0, pl.ds(0, n_x - 1)], ssem.at[4, c])
        wait_bytes(out_ref.at[c, 0], ssem.at[5, c])


def on_device(
    embed_table,
    owner_shard,
    local_row,
    lengths,
    spd_bucket,
    degree_bucket,
    w_query,
    w_key,
    w_value,
    w_out,
    spd_bias,
    degree_bias,
    cotangent,
):
    n_batch, n_node = lax.axis_size("batch"), lax.axis_size("node")
    n_z = Z_SIZE
    n_x = n_batch // n_z
    _, slots, feature_dim = cotangent.shape
    table_rows = embed_table.shape[0]
    width = feature_dim // n_node
    half = width // 2
    heads = width // HEAD_DIM
    entries = n_batch * PAIR_ROWS
    vmem = pl.BlockSpec(memory_space=pltpu.VMEM)
    smem = pl.BlockSpec(memory_space=pltpu.SMEM)
    anywhere = pl.BlockSpec(memory_space=pl.ANY)
    shaped = jax.ShapeDtypeStruct
    dma = pltpu.SemaphoreType.DMA

    rows, reqs, dest = pl.pallas_call(
        functools.partial(fetch_kernel, n_batch, n_node),
        out_shape=(
            shaped((n_node, slots, width), BF16),
            shaped((2, n_batch, 1, 128), I32),
            shaped((1, slots), I32),
        ),
        in_specs=[vmem, vmem, anywhere],
        out_specs=(vmem, vmem, vmem),
        scratch_shapes=[
            pltpu.VMEM((table_rows, width), BF16),
            pltpu.VMEM((n_batch, 1, 128), I32),
            pltpu.VMEM((entries, 128), I32),
            pltpu.VMEM((n_batch, PAIR_ROWS, width), BF16),
            pltpu.VMEM((n_batch, PAIR_ROWS, width), BF16),
            dma,
            dma((4,)),
            dma((4,)),
        ],
        compiler_params=pltpu.CompilerParams(
            collective_id=0, has_side_effects=True, vmem_limit_bytes=24 * 2**20
        ),
        name="fetch_rows",
    )(owner_shard.reshape(1, slots), local_row.reshape(1, slots), embed_table)

    grads, d_rows, small = pl.pallas_call(
        layer_kernel,
        out_shape=(
            shaped((4, 2, 4, feature_dim // 8, width), BF16),
            shaped((n_node, slots, width), BF16),
            shaped((8, heads * (NSPD + NDEG)), F32),
        ),
        in_specs=[smem, smem, smem] + [vmem] * 8,
        out_specs=(vmem, vmem, vmem),
        scratch_shapes=[
            pltpu.VMEM((heads, slots, slots), F32),
            pltpu.VMEM((heads, slots, slots), F32),
            pltpu.VMEM((heads * (NSPD + NDEG), 128), F32),
        ],
        compiler_params=pltpu.CompilerParams(vmem_limit_bytes=48 * 2**20),
        name="layer",
    )(
        lengths,
        spd_bias,
        degree_bias,
        rows,
        spd_bucket.reshape(slots, slots),
        degree_bucket,
        cotangent.reshape(slots, feature_dim),
        w_query,
        w_key,
        w_value,
        w_out,
    )

    chunks = 4
    quarter = feature_dim // 8
    piece = quarter // n_z
    small_shape = small.shape
    out, table_grad, small = pl.pallas_call(
        functools.partial(reduce_kernel, n_batch, n_node),
        out_shape=(
            shaped((chunks, 2, n_x, n_z, piece, width), BF16),
            shaped((table_rows, half), F32),
            shaped(small_shape, F32),
        ),
        in_specs=[vmem] * 5,
        out_specs=(vmem, vmem, vmem),
        scratch_shapes=[
            pltpu.VMEM((chunks, n_x, quarter, width), BF16),
            pltpu.VMEM((chunks, n_x, quarter, width), BF16),
            pltpu.VMEM((chunks, n_x, quarter, width), BF16),
            pltpu.VMEM((chunks, n_z, piece, width), BF16),
            pltpu.VMEM((chunks, n_z, piece, width), BF16),
            pltpu.VMEM((n_node, slots, width), BF16),
            pltpu.VMEM((2, n_batch, PAIR_ROWS, half), BF16),
            pltpu.VMEM((n_batch, PAIR_ROWS, half), BF16),
            pltpu.VMEM((2, n_batch, PAIR_ROWS, half), BF16),
            pltpu.VMEM(small_shape, F32),
            pltpu.VMEM((n_x,) + small_shape, F32),
            pltpu.VMEM((n_z,) + small_shape, F32),
            pltpu.VMEM((entries, 128), I32),
            dma((6, chunks)),
            dma((6, chunks)),
            dma((3,)),
            dma((3,)),
            dma((3,)),
            dma((3,)),
        ],
        compiler_params=pltpu.CompilerParams(
            collective_id=1, has_side_effects=True, vmem_limit_bytes=48 * 2**20
        ),
        name="reduce_gradients",
    )(grads, d_rows, small, dest, reqs)

    out = out.reshape(chunks, feature_dim, width).astype(F32)
    by_bucket = small[0].reshape(heads, NSPD + NDEG).T
    out_grad = out[0].reshape(n_node, width, width).transpose(1, 0, 2).reshape(width, feature_dim)
    return (
        table_grad,
        out[3],
        out[2],
        out[1],
        out_grad,
        by_bucket[:NSPD],
        by_bucket[NSPD:],
    )


def solution(mesh):
    placed = (
        P("batch", None),
        P(("batch", "replica"), None, None),
        P(("batch", "replica"), None),
        P(("batch", "replica")),
        P(("batch", "replica"), None, None),
        P(("batch", "replica"), None),
        P(None, "node"),
        P(None, "node"),
        P(None, "node"),
        P("node", None),
        P(None, "node"),
        P(None, "node"),
        P(("batch", "replica"), None, None),
    )
    return jax.shard_map(
        on_device,
        mesh=mesh,
        in_specs=placed,
        out_specs=(
            P("batch", ("node", "replica")),
            P(None, "node"),
            P(None, "node"),
            P(None, "node"),
            P("node", None),
            P(None, "node"),
            P(None, "node"),
        ),
        check_vma=False,
    )
```

```python
import functools

import jax
import jax.numpy as jnp
from jax import lax
from jax.experimental import pallas as pl
from jax.experimental.pallas import tpu as pltpu
from jax.sharding import PartitionSpec as P

HEAD_DIM = 64
NSPD = 16
NDEG = 32
EPS = 1e-05
PAIR_ROWS = 16
Z_SIZE = 8
MESH = pl.DeviceIdType.MESH
F32 = jnp.float32
BF16 = jnp.bfloat16
I32 = jnp.int32


def iota(shape, dim):
    return lax.broadcasted_iota(I32, shape, dim)


def dot(a, b, ca=1, cb=0, precision=None):
    return lax.dot_general(
        a, b, (((ca,), (cb,)), ((), ())), preferred_element_type=F32, precision=precision
    )


def remote(src, dst, send_sem, recv_sem, **where):
    return pltpu.make_async_remote_copy(
        src_ref=src,
        dst_ref=dst,
        send_sem=send_sem,
        recv_sem=recv_sem,
        device_id=where,
        device_id_type=MESH,
    )


def wait_bytes(ref, sem):
    pltpu.make_async_copy(ref, ref, sem).wait()


def train_kernel(
    n_batch,
    n_node,
    length_ref,
    spd_bias_ref,
    deg_bias_ref,
    owner_hbm,
    local_hbm,
    deg_hbm,
    table_hbm,
    spd_hbm,
    cot_hbm,
    wo_hbm,
    wq_hbm,
    wk_hbm,
    wv_hbm,
    out_hbm,
    table_hbm_out,
    small_hbm,
    owner_v,
    local_v,
    deg_v,
    table_v,
    spd_v,
    cot_v,
    wo_v,
    wq_v,
    wk_v,
    wv_v,
    ask,
    reqs,
    spread,
    rows_send,
    rows_recv,
    rows,
    dest_v,
    bias,
    d_att_v,
    probs_v,
    d_scores,
    sums,
    small,
    grads,
    d_rows_v,
    core_in,
    core_sum,
    x1_in,
    x2_in,
    x_sum,
    z_in,
    y_in,
    pack,
    to_core,
    table_in,
    small_core,
    small_x,
    small_z,
    out_ref,
    table_ref,
    small_out,
    lsem,
    gs,
    gr,
    ssem,
    rsem,
    fs,
    fr,
    ts,
    tr,
    wsem,
):
    me_b, me_n, me_r = lax.axis_index("batch"), lax.axis_index("node"), lax.axis_index("replica")
    n_z = Z_SIZE
    n_x = n_batch // n_z
    me_x, me_z = me_b // n_z, me_b % n_z
    other = 1 - me_r
    up, down, across_x = lax.rem(me_x + 1, n_x), lax.rem(me_x + 3, n_x), lax.rem(me_x + 2, n_x)
    slots, feature_dim = cot_v.shape
    table_rows, width = table_v.shape
    heads = width // HEAD_DIM
    blocks = feature_dim // width
    half = width // 2
    entries = n_batch * PAIR_ROWS
    chunks = out_ref.shape[0]
    piece = out_ref.shape[4]
    quarter = n_z * piece
    copies = 2.0 * n_batch
    scale = HEAD_DIM ** (-0.5)
    step = 32
    z_order = (4, 3, 5, 2, 6, 1, 7)
    barrier = pltpu.get_barrier_semaphore()

    def signal_batch(j, carry):
        p = lax.rem(me_b + j, n_batch)
        pl.semaphore_signal(barrier, inc=1, device_id={"batch": p}, device_id_type=MESH)
        return carry

    lax.fori_loop(1, n_batch, signal_batch, 0)
    for j in range(1, n_node):
        p = lax.rem(me_n + j, n_node)
        pl.semaphore_signal(barrier, inc=1, device_id={"node": p}, device_id_type=MESH)
    pl.semaphore_signal(barrier, inc=1, device_id={"replica": other}, device_id_type=MESH)

    columns = pl.ds(pl.multiple_of(me_n * width, width), width)
    loads = [
        pltpu.make_async_copy(src, dst, lsem.at[i])
        for i, (src, dst) in enumerate(
            (
                (owner_hbm, owner_v),
                (local_hbm, local_v),
                (deg_hbm, deg_v),
                (spd_hbm, spd_v),
                (table_hbm.at[:, columns], table_v),
                (cot_hbm, cot_v),
                (wo_hbm, wo_v),
                (wq_hbm, wq_v),
                (wk_hbm, wk_v),
                (wv_hbm, wv_v),
            )
        )
    ]
    for load in loads:
        load.start()

    loads[0].wait()
    loads[1].wait()
    owner_row = owner_v[...]
    across = jnp.broadcast_to(owner_row, (slots, slots))
    owner_down = jnp.transpose(across)
    same = across == owner_down
    r0, r1 = iota((slots, slots), 0), iota((slots, slots), 1)
    rank_row = jnp.sum(jnp.where(same & (r0 < r1), 1.0, 0.0), axis=0, keepdims=True).astype(I32)
    rank_col = jnp.sum(jnp.where(same & (r1 < r0), 1.0, 0.0), axis=1, keepdims=True).astype(I32)
    dest_v[...] = owner_row * PAIR_ROWS + rank_row
    dest_col = owner_down[:, 0:1] * PAIR_ROWS + rank_col

    wanted = local_v[...] + 1
    hit = owner_row == iota((n_batch, slots), 0)
    high = jnp.where(hit, (wanted // 32).astype(F32), 0.0).astype(BF16)
    low = jnp.where(hit, (wanted % 32).astype(F32), 0.0).astype(BF16)
    at_rank = jnp.where(rank_col == iota((slots, 128), 1), 1.0, 0.0).astype(BF16)
    listed = (dot(high, at_rank) * 32.0 + dot(low, at_rank)).astype(I32)
    for o in range(n_batch):
        ask[o] = listed[o : o + 1, :]

    pl.semaphore_wait(barrier, n_batch - 1 + n_node - 1 + 1)

    def send_ask(j, carry):
        p = lax.rem(me_b + j, n_batch)
        remote(ask.at[p], reqs.at[me_r, me_b], gs.at[0], gr.at[0], batch=p).start()
        return carry

    lax.fori_loop(1, n_batch, send_ask, 0)
    reqs[me_r, me_b] = ask[me_b]

    loads[2].wait()
    loads[3].wait()

    def bias_block(i, carry):
        at = pl.ds(pl.multiple_of(i * step, step), step)
        bucket = spd_v[at, :]
        terms = [jnp.full(bucket.shape, spd_bias_ref[h, 0], F32) for h in range(heads)]
        for b in range(1, NSPD):
            is_b = bucket == b
            terms = [jnp.where(is_b, spd_bias_ref[h, b], terms[h]) for h in range(heads)]
        for h in range(heads):
            bias[h, at, :] = terms[h]
        return carry

    lax.fori_loop(0, slots // step, bias_block, 0)
    place = jnp.where(iota((slots, entries), 1) == dest_col, 1.0, 0.0).astype(BF16)

    loads[4].wait()
    wait_bytes(ask.at[pl.ds(0, n_batch - 1)], gr.at[0])
    remote(reqs.at[me_r], reqs.at[me_r], gs.at[1], gr.at[1], replica=other).start()
    group = n_z * PAIR_ROWS
    mine = iota((group, 128), 1) == iota((group, 128), 0) % PAIR_ROWS
    for dx in (2, 1, 3, 0):
        first = lax.rem(me_x + dx, n_x) * n_z
        for k in range(n_z):
            spread[k * PAIR_ROWS : (k + 1) * PAIR_ROWS, :] = jnp.broadcast_to(
                reqs[me_r, first + k], (PAIR_ROWS, 128)
            )
        listed = spread[0:group, :].astype(F32)
        target = jnp.sum(jnp.where(mine, listed, 0.0), axis=1, keepdims=True).astype(I32) - 1
        pick = jnp.where(iota((group, table_rows), 1) == target, 1.0, 0.0).astype(BF16)
        rows_send[pl.ds(first, n_z)] = (
            dot(pick, table_v[...]).astype(BF16).reshape(n_z, PAIR_ROWS, width)
        )
        for dz in z_order + ((0,) if dx else ()):
            p = first + lax.rem(me_z + dz, n_z)
            remote(rows_send.at[p], rows_recv.at[me_b], gs.at[2], gr.at[2], batch=p).start()
    rows_recv[me_b] = rows_send[me_b]

    loads[5].wait()
    loads[6].wait()
    length = length_ref[0]
    d_masked = jnp.where(
        iota((slots, feature_dim), 0) < length, cot_v[...].astype(F32), 0.0
    ).astype(BF16)
    cot_v[...] = d_masked
    d_att_v[...] = dot(d_masked, wo_v[...], 1, 1).astype(BF16)
    degree = deg_v[...]
    deg_terms = []
    for h in range(heads):
        term = jnp.full(degree.shape, deg_bias_ref[h, 0], F32)
        for b in range(1, NDEG):
            term = jnp.where(degree == b, deg_bias_ref[h, b], term)
        deg_terms.append(term)

    wait_bytes(rows_recv.at[pl.ds(0, n_batch - 1)], gr.at[2])
    rows[me_n] = dot(place, rows_recv[...].reshape(entries, width)).astype(BF16)
    for j in (2, 1, 3):
        p = lax.rem(me_n + j, n_node)
        remote(rows.at[me_n], rows.at[me_n], gs.at[3], gr.at[3], node=p).start()
    for load in loads[7:]:
        load.wait()
    wait_bytes(rows.at[pl.ds(0, n_node - 1)], gr.at[3])

    def core_send(c):
        remote(grads.at[c, other], core_in.at[c], ssem.at[0, c], rsem.at[0, c], replica=other).start()

    def x_far(c):
        wait_bytes(core_in.at[c], rsem.at[0, c])
        core_sum[c] = (grads[c, me_r].astype(F32) + core_in[c].astype(F32)).astype(BF16)
        for d, to in enumerate((up, down)):
            remote(
                core_sum.at[c, across_x, pl.ds(d * (quarter // 2), quarter // 2)],
                x1_in.at[c, d],
                ssem.at[1, c],
                rsem.at[1, c],
                batch=to * n_z + me_z,
            ).start()

    def x_near(c):
        wait_bytes(x1_in.at[c], rsem.at[1, c])
        for d, to in enumerate((up, down)):
            part = pl.ds(d * (quarter // 2), quarter // 2)
            core_sum[c, to, part] = (
                core_sum[c, to, part].astype(F32) + x1_in[c, d].astype(F32)
            ).astype(BF16)
            remote(
                core_sum.at[c, to],
                x2_in.at[c, d],
                ssem.at[2, c],
                rsem.at[2, c],
                batch=to * n_z + me_z,
            ).start()

    def z_send(c):
        wait_bytes(x2_in.at[c], rsem.at[2, c])
        total = core_sum[c, me_x].astype(F32) + x2_in[c, 0].astype(F32) + x2_in[c, 1].astype(F32)
        x_sum[c] = total.astype(BF16).reshape(n_z, piece, width)
        for j in z_order:
            p = lax.rem(me_z + j, n_z)
            remote(
                x_sum.at[c, p],
                z_in.at[c, me_z],
                ssem.at[3, c],
                rsem.at[3, c],
                batch=me_x * n_z + p,
            ).start()
        z_in[c, me_z] = x_sum[c, me_z]

    def z_back(c):
        wait_bytes(z_in.at[c, pl.ds(0, n_z - 1)], rsem.at[3, c])
        total = z_in[c, 0].astype(F32)
        for z in range(1, n_z):
            total = total + z_in[c, z].astype(F32)
        out_ref[c, me_r, me_x, me_z] = (total * (1.0 / copies)).astype(BF16)
        done = out_ref.at[c, me_r, me_x, me_z]
        for j in z_order:
            p = lax.rem(me_z + j, n_z)
            remote(done, done, ssem.at[4, c], rsem.at[4, c], batch=me_x * n_z + p).start()

    def x_back(c):
        wait_bytes(out_ref.at[c, 0, 0, pl.ds(0, n_z - 1)], rsem.at[4, c])
        done = out_ref.at[c, me_r, me_x]
        for to in (up, down):
            remote(done, done, ssem.at[5, c], rsem.at[5, c], batch=to * n_z + me_z).start()

    def x_pass(c):
        wait_bytes(out_ref.at[c, 0, pl.ds(0, 2)], rsem.at[5, c])
        for d, (source, to) in enumerate(((down, up), (up, down))):
            done = out_ref.at[c, me_r, source, pl.ds(d * (n_z // 2), n_z // 2)]
            remote(done, done, ssem.at[6, c], rsem.at[6, c], batch=to * n_z + me_z).start()

    def core_back(c):
        wait_bytes(out_ref.at[c, 0, 0], rsem.at[6, c])
        done = out_ref.at[c, me_r]
        remote(done, done, ssem.at[7, c], rsem.at[7, c], replica=other).start()

    x = jnp.concatenate([rows[b] for b in range(blocks)], axis=1).astype(F32)
    centred = x - jnp.mean(x, axis=1, keepdims=True)
    inv_std = lax.rsqrt(jnp.mean(centred * centred, axis=1, keepdims=True) + EPS)
    x_hat = centred * inv_std
    normed = x_hat.astype(BF16)
    queries = dot(normed, wq_v[...]).astype(BF16)
    keys = dot(normed, wk_v[...]).astype(BF16)
    values = dot(normed, wv_v[...]).astype(BF16)
    normed_t = jnp.transpose(normed)
    d_att = d_att_v[...]

    lane_head = iota((slots, width), 1) // HEAD_DIM

    def only(h, a):
        return jnp.where(lane_head == h, a, jnp.zeros_like(a))

    valid = iota((slots, slots), 1) < length
    attended = jnp.zeros((slots, width), F32)
    d_values = jnp.zeros((slots, width), F32)
    for h in range(heads):
        scores = dot(only(h, queries), keys, 1, 1) * scale + bias[h] + deg_terms[h]
        scores = jnp.where(valid, scores, -jnp.inf)
        exps = jnp.exp(scores - jnp.max(scores, axis=1, keepdims=True))
        probs = exps / jnp.sum(exps, axis=1, keepdims=True)
        probs_v[h] = probs
        probs_b = probs.astype(BF16)
        attended = attended + dot(probs_b, only(h, values))
        d_values = d_values + dot(probs_b, only(h, d_att), 0, 0)
    out_part = dot(attended.astype(BF16), cot_v[...], 0, 0).astype(BF16)
    for b in range(blocks):
        for k in range(2):
            grads[0, b // 2, 2 * (b % 2) + k] = out_part[
                k * quarter : (k + 1) * quarter, b * width : (b + 1) * width
            ]
    core_send(0)
    halves = (2, n_x, quarter, width)
    d_values = d_values.astype(BF16)
    grads[1] = dot(normed_t, d_values).astype(BF16).reshape(halves)
    core_send(1)

    d_queries = jnp.zeros((slots, width), F32)
    d_keys = jnp.zeros((slots, width), F32)
    for h in range(heads):
        probs = probs_v[h]
        d_probs = dot(only(h, d_att), values, 1, 1)
        ds = probs * (d_probs - jnp.sum(probs * d_probs, axis=1, keepdims=True))
        d_scores[h] = ds
        ds_b = ds.astype(BF16)
        d_queries = d_queries + dot(ds_b, only(h, keys))
        d_keys = d_keys + dot(ds_b, only(h, queries), 0, 0)
    d_queries = (d_queries * scale).astype(BF16)
    d_keys = (d_keys * scale).astype(BF16)
    x_far(0)
    grads[2] = dot(normed_t, d_keys).astype(BF16).reshape(halves)
    core_send(2)
    x_far(1)
    grads[3] = dot(normed_t, d_queries).astype(BF16).reshape(halves)
    core_send(3)
    x_near(0)

    d_normed = (
        dot(d_queries, wq_v[...], 1, 1)
        + dot(d_keys, wk_v[...], 1, 1)
        + dot(d_values, wv_v[...], 1, 1)
    )
    lead = jnp.where(me_n == 0, 1.0, 0.0)
    d_rows = lead * cot_v[...].astype(F32) + inv_std * (
        d_normed
        - jnp.mean(d_normed, axis=1, keepdims=True)
        - x_hat * jnp.mean(d_normed * x_hat, axis=1, keepdims=True)
    )
    for b in range(blocks):
        d_rows_v[b] = d_rows[:, b * width : (b + 1) * width].astype(BF16)
    for j in (2, 1, 3):
        p = lax.rem(me_n + j, n_node)
        remote(d_rows_v.at[p], y_in.at[me_n], fs.at[0], fr.at[0], node=p).start()
    y_in[me_n] = d_rows_v[me_n]

    def bucket_sums(h):
        def spd_block(i, totals):
            at = pl.ds(pl.multiple_of(i * step, step), step)
            bucket, ds = spd_v[at, :], d_scores[h, at, :]
            new = []
            for b in range(NSPD):
                kept = jnp.where(bucket == b, ds, 0.0)
                kept = kept[:, :128] + kept[:, 128:]
                new.append(totals[b] + (kept[0:8] + kept[8:16]) + (kept[16:24] + kept[24:32]))
            return tuple(new)

        totals = lax.fori_loop(
            0, slots // step, spd_block, tuple(jnp.zeros((8, 128), F32) for _ in range(NSPD))
        )
        sums[h * 128 : (h + 1) * 128, :] = jnp.zeros((128, 128), F32)
        for b in range(NSPD):
            at = h * 128 + b
            sums[at : at + 1, :] = jnp.sum(totals[b], axis=0, keepdims=True)
        by_key = jnp.sum(d_scores[h], axis=0, keepdims=True)
        kept = jnp.where(degree == iota((NDEG, slots), 0), by_key, 0.0)
        at = h * 128 + NSPD
        sums[at : at + NDEG, :] = kept[:, :128] + kept[:, 128:]

    x_far(2)
    x_near(1)
    x_far(3)
    z_send(0)
    bucket_sums(0)
    x_near(2)
    z_send(1)
    bucket_sums(1)
    x_near(3)

    lists = jnp.where(iota((entries, slots), 0) == dest_v[...], 1.0, 0.0).astype(BF16)
    wait_bytes(y_in.at[pl.ds(0, n_node - 1)], fr.at[0])
    d_rows = y_in[0].astype(F32)
    for n in range(1, n_node):
        d_rows = d_rows + y_in[n].astype(F32)
    packed = dot(lists, d_rows.astype(BF16)).astype(BF16)
    left, right = packed[:, :half], packed[:, half:]
    shape = (n_batch, PAIR_ROWS, half)
    to_core[...] = jnp.where(me_r == 0, right, left).reshape(shape)
    remote(to_core, pack.at[me_r], fs.at[1], fr.at[1], replica=other).start()
    pack[me_r] = jnp.where(me_r == 0, left, right).reshape(shape)

    z_send(2)
    z_back(0)
    bucket_sums(2)
    wait_bytes(to_core, fr.at[1])
    for dx in (2, 1, 3, 0):
        first = lax.rem(me_x + dx, n_x) * n_z
        for dz in z_order + ((0,) if dx else ()):
            p = first + lax.rem(me_z + dz, n_z)
            remote(pack.at[:, p], table_in.at[:, me_b], fs.at[2], fr.at[2], batch=p).start()
    table_in[:, me_b] = pack[:, me_b]
    z_send(3)
    z_back(1)
    bucket_sums(3)
    totals = dot(jnp.ones((8, 128), F32), sums[...], 1, 1, precision=lax.Precision.HIGHEST)
    small[...] = jnp.zeros_like(small)
    for h in range(heads):
        small[h : h + 1, :] = totals[0:1, h * 128 : (h + 1) * 128]
    remote(small, small_core, ts.at[0], tr.at[0], replica=other).start()
    z_back(2)
    x_back(0)
    wait_bytes(small_core, tr.at[0])
    small_x[me_x] = small[...] + small_core[...]
    for j in (2, 1, 3):
        p = lax.rem(me_x + j, n_x)
        remote(
            small_x.at[me_x], small_x.at[me_x], ts.at[1], tr.at[1], batch=p * n_z + me_z
        ).start()
    z_back(3)
    x_back(1)

    wait_bytes(reqs.at[0], gr.at[1])
    mine = iota((entries, 128), 1) == iota((entries, 128), 0) % PAIR_ROWS
    targets = []
    for r in range(2):
        for p in range(n_batch):
            spread[p * PAIR_ROWS : (p + 1) * PAIR_ROWS, :] = jnp.broadcast_to(
                reqs[r, p], (PAIR_ROWS, 128)
            )
        target = jnp.sum(jnp.where(mine, spread[...].astype(F32), 0.0), axis=1, keepdims=True) - 1.0
        flat = jnp.transpose(jnp.broadcast_to(target, (entries, 128)))[0:1, :].astype(I32)
        targets.append(flat)
    x_pass(0)
    x_back(2)
    wait_bytes(small_x.at[pl.ds(0, n_x - 1)], tr.at[1])
    total = small_x[0]
    for x in range(1, n_x):
        total = total + small_x[x]
    small_z[me_z] = total
    for j in z_order:
        p = lax.rem(me_z + j, n_z)
        remote(
            small_z.at[me_z], small_z.at[me_z], ts.at[2], tr.at[2], batch=me_x * n_z + p
        ).start()
    x_pass(1)
    x_back(3)
    core_back(0)

    row = iota((table_rows, entries), 0)
    scatter = [jnp.where(row == t, 1.0, 0.0).astype(BF16) for t in targets]
    wait_bytes(table_in.at[:, pl.ds(0, n_batch - 1)], fr.at[2])
    table_ref[...] = dot(scatter[0], table_in[0].reshape(entries, half)) + dot(
        scatter[1], table_in[1].reshape(entries, half)
    )
    writes = [pltpu.make_async_copy(table_ref, table_hbm_out, wsem.at[chunks])]
    writes[0].start()
    x_pass(2)
    core_back(1)
    x_pass(3)
    core_back(2)
    wait_bytes(small_z.at[pl.ds(0, n_z - 1)], tr.at[2])
    total = small_z[0]
    for z in range(1, n_z):
        total = total + small_z[z]
    small_out[...] = total * (1.0 / copies)
    core_back(3)
    writes.append(pltpu.make_async_copy(small_out, small_hbm, wsem.at[chunks + 1]))
    writes[-1].start()
    for c in range(chunks):
        wait_bytes(out_ref.at[c, 0], rsem.at[7, c])
        writes.append(pltpu.make_async_copy(out_ref.at[c], out_hbm.at[c], wsem.at[c]))
        writes[-1].start()

    wait_bytes(ask.at[pl.ds(0, n_batch - 1)], gs.at[0])
    wait_bytes(reqs.at[0], gs.at[1])
    wait_bytes(rows_send.at[pl.ds(0, n_batch - 1)], gs.at[2])
    wait_bytes(rows.at[pl.ds(0, n_node - 1)], gs.at[3])
    wait_bytes(y_in.at[pl.ds(0, n_node - 1)], fs.at[0])
    wait_bytes(to_core, fs.at[1])
    wait_bytes(table_in.at[:, pl.ds(0, n_batch - 1)], fs.at[2])
    wait_bytes(small_core, ts.at[0])
    wait_bytes(small_x.at[pl.ds(0, n_x - 1)], ts.at[1])
    wait_bytes(small_z.at[pl.ds(0, n_z - 1)], ts.at[2])
    for c in range(chunks):
        wait_bytes(core_in.at[c], ssem.at[0, c])
        wait_bytes(x1_in.at[c], ssem.at[1, c])
        wait_bytes(x2_in.at[c], ssem.at[2, c])
        wait_bytes(z_in.at[c, pl.ds(0, n_z - 1)], ssem.at[3, c])
        wait_bytes(out_ref.at[c, 0, 0, pl.ds(0, n_z - 1)], ssem.at[4, c])
        wait_bytes(out_ref.at[c, 0, pl.ds(0, 2)], ssem.at[5, c])
        wait_bytes(out_ref.at[c, 0, 0], ssem.at[6, c])
        wait_bytes(out_ref.at[c, 0], ssem.at[7, c])
    for write in writes:
        write.wait()


def finish_kernel(
    sums_hbm,
    table_hbm,
    small_hbm,
    table_out,
    query_out,
    key_out,
    value_out,
    out_out,
    spd_out,
    deg_out,
    sums_v,
    small_v,
    table_v,
    wide,
    outer,
    rsem,
    wsem,
):
    chunks = sums_v.shape[0]
    width = outer.shape[0]
    reads = [
        pltpu.make_async_copy(sums_hbm.at[c], sums_v.at[c], rsem.at[c]) for c in range(chunks)
    ]
    reads.append(pltpu.make_async_copy(small_hbm, small_v, rsem.at[chunks]))
    reads.append(pltpu.make_async_copy(table_hbm, table_v, rsem.at[chunks + 1]))
    for read in reads:
        read.start()
    reads[0].wait()
    step = 64
    steps = width // step

    def widen_outer(i, carry):
        at = pl.ds(pl.multiple_of(i * step, step), step)
        for b in range(outer.shape[1] // width):
            row = pl.ds(pl.multiple_of(i * step + b * width, step), step)
            outer[at, b * width : (b + 1) * width] = sums_v[0, row].astype(F32)
        return carry

    lax.fori_loop(0, steps, widen_outer, 0)
    writes = [pltpu.make_async_copy(outer, out_out, wsem.at[0])]
    writes[0].start()
    for c, out in ((1, value_out), (2, key_out), (3, query_out)):
        reads[c].wait()

        def widen(i, carry, c=c):
            at = pl.ds(pl.multiple_of(i * width, width), width)
            wide[c - 1, at] = sums_v[c, at].astype(F32)
            return carry

        lax.fori_loop(0, sums_v.shape[1] // width, widen, 0)
        writes.append(pltpu.make_async_copy(wide.at[c - 1], out, wsem.at[c]))
        writes[-1].start()
    reads[chunks + 1].wait()
    writes.append(pltpu.make_async_copy(table_v, table_out, wsem.at[chunks]))
    writes[-1].start()
    reads[chunks].wait()
    heads = spd_out.shape[0]
    spd_out[...] = small_v[0:heads, 0:NSPD]
    deg_out[...] = small_v[0:heads, NSPD : NSPD + NDEG]
    for write in writes:
        write.wait()


def on_device(
    embed_table,
    owner_shard,
    local_row,
    lengths,
    spd_bucket,
    degree_bucket,
    w_query,
    w_key,
    w_value,
    w_out,
    spd_bias,
    degree_bias,
    cotangent,
):
    n_batch, n_node = lax.axis_size("batch"), lax.axis_size("node")
    n_z = Z_SIZE
    n_x = n_batch // n_z
    _, slots, feature_dim = cotangent.shape
    table_rows = embed_table.shape[0]
    width = feature_dim // n_node
    half = width // 2
    heads = width // HEAD_DIM
    entries = n_batch * PAIR_ROWS
    chunks = 4
    quarter = feature_dim // (2 * n_x)
    piece = quarter // n_z
    vmem = pl.BlockSpec(memory_space=pltpu.VMEM)
    smem = pl.BlockSpec(memory_space=pltpu.SMEM)
    hbm = pl.BlockSpec(memory_space=pltpu.HBM)
    shaped = jax.ShapeDtypeStruct
    dma = pltpu.SemaphoreType.DMA
    v = pltpu.VMEM

    sums, table_grad, small = pl.pallas_call(
        functools.partial(train_kernel, n_batch, n_node),
        out_shape=(
            shaped((chunks, 2, n_x, n_z, piece, width), BF16),
            shaped((table_rows, half), F32),
            shaped((8, 128), F32),
        ),
        in_specs=[smem] * 3 + [hbm] * 10,
        out_specs=(hbm, hbm, hbm),
        scratch_shapes=[
            v((1, slots), I32),
            v((1, slots), I32),
            v((1, slots), I32),
            v((table_rows, width), BF16),
            v((slots, slots), I32),
            v((slots, feature_dim), BF16),
            v((width, feature_dim), BF16),
            v((feature_dim, width), BF16),
            v((feature_dim, width), BF16),
            v((feature_dim, width), BF16),
            v((n_batch, 1, 128), I32),
            v((2, n_batch, 1, 128), I32),
            v((entries, 128), I32),
            v((n_batch, PAIR_ROWS, width), BF16),
            v((n_batch, PAIR_ROWS, width), BF16),
            v((n_node, slots, width), BF16),
            v((1, slots), I32),
            v((heads, slots, slots), F32),
            v((slots, width), BF16),
            v((heads, slots, slots), F32),
            v((heads, slots, slots), F32),
            v((heads * 128, 128), F32),
            v((8, 128), F32),
            v((chunks, 2, n_x, quarter, width), BF16),
            v((n_node, slots, width), BF16),
            v((chunks, n_x, quarter, width), BF16),
            v((chunks, n_x, quarter, width), BF16),
            v((chunks, 2, quarter // 2, width), BF16),
            v((chunks, 2, quarter, width), BF16),
            v((chunks, n_z, piece, width), BF16),
            v((chunks, n_z, piece, width), BF16),
            v((n_node, slots, width), BF16),
            v((2, n_batch, PAIR_ROWS, half), BF16),
            v((n_batch, PAIR_ROWS, half), BF16),
            v((2, n_batch, PAIR_ROWS, half), BF16),
            v((8, 128), F32),
            v((n_x, 8, 128), F32),
            v((n_z, 8, 128), F32),
            v((chunks, 2, n_x, n_z, piece, width), BF16),
            v((table_rows, half), F32),
            v((8, 128), F32),
            dma((10,)),
            dma((4,)),
            dma((4,)),
            dma((8, chunks)),
            dma((8, chunks)),
            dma((3,)),
            dma((3,)),
            dma((3,)),
            dma((3,)),
            dma((chunks + 2,)),
        ],
        compiler_params=pltpu.CompilerParams(
            collective_id=0, has_side_effects=True, vmem_limit_bytes=61 * 2**20
        ),
        name="layer_and_exchanges",
    )(
        lengths,
        spd_bias.T,
        degree_bias.T,
        owner_shard.reshape(1, slots),
        local_row,
        degree_bucket,
        embed_table,
        spd_bucket.reshape(slots, slots),
        cotangent.reshape(slots, feature_dim),
        w_out,
        w_query,
        w_key,
        w_value,
    )

    square = shaped((feature_dim, width), F32)
    table_grad, query_grad, key_grad, value_grad, out_grad, spd_grad, degree_grad = pl.pallas_call(
        finish_kernel,
        out_shape=(
            shaped((table_rows, half), F32),
            square,
            square,
            square,
            shaped((width, feature_dim), F32),
            shaped((heads, NSPD), F32),
            shaped((heads, NDEG), F32),
        ),
        in_specs=[hbm] * 3,
        out_specs=(hbm,) * 5 + (vmem, vmem),
        scratch_shapes=[
            v((chunks, feature_dim, width), BF16),
            v((8, 128), F32),
            v((table_rows, half), F32),
            v((3, feature_dim, width), F32),
            v((width, feature_dim), F32),
            dma((chunks + 2,)),
            dma((chunks + 1,)),
        ],
        compiler_params=pltpu.CompilerParams(vmem_limit_bytes=61 * 2**20),
        name="write_outputs",
    )(sums.reshape(chunks, feature_dim, width), table_grad, small)
    return table_grad, query_grad, key_grad, value_grad, out_grad, spd_grad.T, degree_grad.T


def solution(mesh):
    placed = (
        P("batch", None),
        P(("batch", "replica"), None, None),
        P(("batch", "replica"), None),
        P(("batch", "replica")),
        P(("batch", "replica"), None, None),
        P(("batch", "replica"), None),
        P(None, "node"),
        P(None, "node"),
        P(None, "node"),
        P("node", None),
        P(None, "node"),
        P(None, "node"),
        P(("batch", "replica"), None, None),
    )
    return jax.shard_map(
        on_device,
        mesh=mesh,
        in_specs=placed,
        out_specs=(
            P("batch", ("node", "replica")),
            P(None, "node"),
            P(None, "node"),
            P(None, "node"),
            P("node", None),
            P(None, "node"),
            P(None, "node"),
        ),
        check_vma=False,
    )
```

```python
import functools

import jax
import jax.numpy as jnp
from jax import lax
from jax.experimental import pallas as pl
from jax.experimental.pallas import tpu as pltpu
from jax.sharding import PartitionSpec as P

HEAD_DIM = 64
NSPD = 16
NDEG = 32
EPS = 1e-05
PAIR_ROWS = 16
Z_SIZE = 8
MESH = pl.DeviceIdType.MESH
F32 = jnp.float32
BF16 = jnp.bfloat16
I32 = jnp.int32


def iota(shape, dim):
    return lax.broadcasted_iota(I32, shape, dim)


def dot(a, b, ca=1, cb=0, precision=None):
    return lax.dot_general(
        a, b, (((ca,), (cb,)), ((), ())), preferred_element_type=F32, precision=precision
    )


def remote(src, dst, send_sem, recv_sem, **where):
    return pltpu.make_async_remote_copy(
        src_ref=src,
        dst_ref=dst,
        send_sem=send_sem,
        recv_sem=recv_sem,
        device_id=where,
        device_id_type=MESH,
    )


def wait_bytes(ref, sem):
    pltpu.make_async_copy(ref, ref, sem).wait()


def train_kernel(
    n_batch,
    n_node,
    spd_bias_ref,
    deg_bias_ref,
    length_hbm,
    owner_hbm,
    local_hbm,
    deg_hbm,
    table_hbm,
    spd_hbm,
    cot_hbm,
    wo_hbm,
    wq_hbm,
    wk_hbm,
    wv_hbm,
    out_hbm,
    table_hbm_out,
    small_hbm,
    length_ref,
    owner_v,
    local_v,
    deg_v,
    table_v,
    spd_v,
    cot_v,
    wo_v,
    wq_v,
    wk_v,
    wv_v,
    ask,
    reqs,
    spread,
    rows_send,
    rows_recv,
    rows,
    dest_v,
    bias,
    d_att_v,
    probs_v,
    d_scores,
    sums,
    small,
    grads,
    d_rows_v,
    core_in,
    core_sum,
    x_far_in,
    x_in,
    x_sum,
    z_in,
    y_in,
    pack,
    to_core,
    table_in,
    small_core,
    small_x,
    small_z,
    scatter,
    out_ref,
    table_ref,
    small_out,
    lsem,
    gs,
    gr,
    ssem,
    rsem,
    xsem,
    fs,
    fr,
    ts,
    tr,
    wsem,
):
    me_b, me_n, me_r = lax.axis_index("batch"), lax.axis_index("node"), lax.axis_index("replica")
    n_z = Z_SIZE
    n_x = n_batch // n_z
    me_x, me_z = me_b // n_z, me_b % n_z
    other = 1 - me_r
    up, down, across_x = lax.rem(me_x + 1, n_x), lax.rem(me_x + 3, n_x), lax.rem(me_x + 2, n_x)
    slots, feature_dim = cot_v.shape
    table_rows, width = table_v.shape
    heads = width // HEAD_DIM
    blocks = feature_dim // width
    half = width // 2
    entries = n_batch * PAIR_ROWS
    chunks = out_ref.shape[0]
    piece = out_ref.shape[4]
    quarter = n_z * piece
    copies = 2.0 * n_batch
    scale = HEAD_DIM ** (-0.5)
    step = 32
    z_order = (4, 3, 5, 2, 6, 1, 7)
    barrier = pltpu.get_barrier_semaphore()

    def signal_batch(j, carry):
        p = lax.rem(me_b + j, n_batch)
        pl.semaphore_signal(barrier, inc=1, device_id={"batch": p}, device_id_type=MESH)
        return carry

    lax.fori_loop(1, n_batch, signal_batch, 0)
    for j in range(1, n_node):
        p = lax.rem(me_n + j, n_node)
        pl.semaphore_signal(barrier, inc=1, device_id={"node": p}, device_id_type=MESH)
    pl.semaphore_signal(barrier, inc=1, device_id={"replica": other}, device_id_type=MESH)

    columns = pl.ds(pl.multiple_of(me_n * width, width), width)
    loads = [
        pltpu.make_async_copy(src, dst, lsem.at[i])
        for i, (src, dst) in enumerate(
            (
                (owner_hbm, owner_v),
                (local_hbm, local_v),
                (deg_hbm, deg_v),
                (spd_hbm, spd_v),
                (table_hbm.at[:, columns], table_v),
                (cot_hbm, cot_v),
                (wo_hbm, wo_v),
                (wq_hbm, wq_v),
                (wk_hbm, wk_v),
                (wv_hbm, wv_v),
                (length_hbm, length_ref),
            )
        )
    ]
    for load in loads:
        load.start()

    loads[0].wait()
    loads[1].wait()
    owner_row = owner_v[...]
    across = jnp.broadcast_to(owner_row, (slots, slots))
    owner_down = jnp.transpose(across)
    same = across == owner_down
    r0, r1 = iota((slots, slots), 0), iota((slots, slots), 1)
    rank_row = jnp.sum(jnp.where(same & (r0 < r1), 1.0, 0.0), axis=0, keepdims=True).astype(I32)
    rank_col = jnp.sum(jnp.where(same & (r1 < r0), 1.0, 0.0), axis=1, keepdims=True).astype(I32)
    dest_v[...] = owner_row * PAIR_ROWS + rank_row
    dest_col = owner_down[:, 0:1] * PAIR_ROWS + rank_col

    wanted = local_v[...] + 1
    hit = owner_row == iota((n_batch, slots), 0)
    high = jnp.where(hit, (wanted // 32).astype(F32), 0.0).astype(BF16)
    low = jnp.where(hit, (wanted % 32).astype(F32), 0.0).astype(BF16)
    at_rank = jnp.where(rank_col == iota((slots, 128), 1), 1.0, 0.0).astype(BF16)
    listed = (dot(high, at_rank) * 32.0 + dot(low, at_rank)).astype(I32)
    for o in range(n_batch):
        ask[o] = listed[o : o + 1, :]

    pl.semaphore_wait(barrier, n_batch - 1 + n_node - 1 + 1)

    def send_ask(j, carry):
        p = lax.rem(me_b + j, n_batch)
        remote(ask.at[p], reqs.at[me_r, me_b], gs.at[0], gr.at[0], batch=p).start()
        return carry

    lax.fori_loop(1, n_batch, send_ask, 0)
    reqs[me_r, me_b] = ask[me_b]

    loads[2].wait()
    loads[3].wait()

    def bias_block(i, carry):
        at = pl.ds(pl.multiple_of(i * step, step), step)
        bucket = spd_v[at, :]
        terms = [jnp.full(bucket.shape, spd_bias_ref[h, 0], F32) for h in range(heads)]
        for b in range(1, NSPD):
            is_b = bucket == b
            terms = [jnp.where(is_b, spd_bias_ref[h, b], terms[h]) for h in range(heads)]
        for h in range(heads):
            bias[h, at, :] = terms[h]
        return carry

    lax.fori_loop(0, slots // step, bias_block, 0)
    place = jnp.where(iota((slots, entries), 1) == dest_col, 1.0, 0.0).astype(BF16)

    loads[4].wait()
    wait_bytes(ask.at[pl.ds(0, n_batch - 1)], gr.at[0])
    remote(reqs.at[me_r], reqs.at[me_r], gs.at[1], gr.at[1], replica=other).start()
    group = n_z * PAIR_ROWS
    mine = iota((group, 128), 1) == iota((group, 128), 0) % PAIR_ROWS
    for dx in (2, 1, 3, 0):
        first = lax.rem(me_x + dx, n_x) * n_z
        for k in range(n_z):
            spread[k * PAIR_ROWS : (k + 1) * PAIR_ROWS, :] = jnp.broadcast_to(
                reqs[me_r, first + k], (PAIR_ROWS, 128)
            )
        listed = spread[0:group, :].astype(F32)
        target = jnp.sum(jnp.where(mine, listed, 0.0), axis=1, keepdims=True).astype(I32) - 1
        pick = jnp.where(iota((group, table_rows), 1) == target, 1.0, 0.0).astype(BF16)
        rows_send[pl.ds(first, n_z)] = (
            dot(pick, table_v[...]).astype(BF16).reshape(n_z, PAIR_ROWS, width)
        )
        for dz in z_order + ((0,) if dx else ()):
            p = first + lax.rem(me_z + dz, n_z)
            remote(rows_send.at[p], rows_recv.at[me_b], gs.at[2], gr.at[2], batch=p).start()
    rows_recv[me_b] = rows_send[me_b]

    loads[5].wait()
    loads[6].wait()
    loads[10].wait()
    length = length_ref[...]
    d_masked = jnp.where(
        iota((slots, feature_dim), 0) < length, cot_v[...].astype(F32), 0.0
    ).astype(BF16)
    cot_v[...] = d_masked
    d_att_v[...] = dot(d_masked, wo_v[...], 1, 1).astype(BF16)
    degree = deg_v[...]
    deg_terms = []
    for h in range(heads):
        term = jnp.full(degree.shape, deg_bias_ref[h, 0], F32)
        for b in range(1, NDEG):
            term = jnp.where(degree == b, deg_bias_ref[h, b], term)
        deg_terms.append(term)

    wait_bytes(rows_recv.at[pl.ds(0, n_batch - 1)], gr.at[2])
    rows[me_n] = dot(place, rows_recv[...].reshape(entries, width)).astype(BF16)
    for j in (2, 1, 3):
        p = lax.rem(me_n + j, n_node)
        remote(rows.at[me_n], rows.at[me_n], gs.at[3], gr.at[3], node=p).start()
    for load in loads[7:10]:
        load.wait()
    wait_bytes(rows.at[pl.ds(0, n_node - 1)], gr.at[3])

    def core_send(c):
        remote(grads.at[c, other], core_in.at[c], ssem.at[0, c], rsem.at[0, c], replica=other).start()

    first_half, last_half = pl.ds(0, quarter // 2), pl.ds(quarter // 2, quarter // 2)

    def x_far(c):
        wait_bytes(core_in.at[c], rsem.at[0, c])
        core_sum[c] = (grads[c, me_r].astype(F32) + core_in[c].astype(F32)).astype(BF16)
        for d, (to, part) in enumerate(((up, first_half), (down, last_half))):
            remote(
                core_sum.at[c, across_x, part],
                x_far_in.at[c, d],
                ssem.at[1, c],
                rsem.at[1, c],
                batch=to * n_z + me_z,
            ).start()

    def x_share(c, d, to, part):
        remote(
            core_sum.at[c, to, part],
            x_in.at[c, d, part],
            ssem.at[6, c],
            rsem.at[6, c],
            batch=to * n_z + me_z,
        ).start()

    def x_own(c):
        x_share(c, 0, up, last_half)
        x_share(c, 1, down, first_half)

    def x_near(c):
        wait_bytes(x_far_in.at[c], rsem.at[1, c])
        for d, (to, part) in enumerate(((up, first_half), (down, last_half))):
            core_sum[c, to, part] = (
                core_sum[c, to, part].astype(F32) + x_far_in[c, d].astype(F32)
            ).astype(BF16)
            x_share(c, d, to, part)

    def z_send(c):
        wait_bytes(x_in.at[c], rsem.at[6, c])
        total = core_sum[c, me_x].astype(F32) + x_in[c, 0].astype(F32) + x_in[c, 1].astype(F32)
        x_sum[c] = total.astype(BF16).reshape(n_z, piece, width)
        for j in z_order:
            p = lax.rem(me_z + j, n_z)
            remote(
                x_sum.at[c, p],
                z_in.at[c, me_z],
                ssem.at[2, c],
                rsem.at[2, c],
                batch=me_x * n_z + p,
            ).start()
        z_in[c, me_z] = x_sum[c, me_z]

    def z_back(c):
        wait_bytes(z_in.at[c, pl.ds(0, n_z - 1)], rsem.at[2, c])
        total = z_in[c, 0].astype(F32)
        for z in range(1, n_z):
            total = total + z_in[c, z].astype(F32)
        out_ref[c, me_r, me_x, me_z] = (total * (1.0 / copies)).astype(BF16)
        done = out_ref.at[c, me_r, me_x, me_z]
        for j in z_order:
            p = lax.rem(me_z + j, n_z)
            remote(done, done, ssem.at[3, c], rsem.at[3, c], batch=me_x * n_z + p).start()

    def core_back(c, x):
        done = out_ref.at[c, me_r, x]
        remote(done, done, ssem.at[5, c], rsem.at[5, c], replica=other).start()

    low, high = pl.ds(0, n_z // 2), pl.ds(n_z // 2, n_z // 2)

    def x_give(c, k, source, part, to):
        done = out_ref.at[c, me_r, source, part]
        remote(done, done, ssem.at[4, c], xsem.at[k, c], batch=to * n_z + me_z).start()

    def x_back(c):
        wait_bytes(out_ref.at[c, 0, 0, pl.ds(0, n_z - 1)], rsem.at[3, c])
        x_give(c, 0, me_x, low, up)
        x_give(c, 1, me_x, high, down)
        x_give(c, 2, me_x, high, up)
        x_give(c, 3, me_x, low, down)

    def x_pass(c):
        wait_bytes(out_ref.at[c, 0, 0, low], xsem.at[0, c])
        x_give(c, 4, down, low, up)
        wait_bytes(out_ref.at[c, 0, 0, low], xsem.at[1, c])
        x_give(c, 4, up, high, down)

    def x_done(c):
        wait_bytes(out_ref.at[c, 0, 0, low], xsem.at[2, c])
        core_back(c, down)
        wait_bytes(out_ref.at[c, 0, 0, low], xsem.at[3, c])
        core_back(c, up)

    def x_last(c):
        wait_bytes(out_ref.at[c, 0, 0], xsem.at[4, c])
        core_back(c, across_x)

    x = jnp.concatenate([rows[b] for b in range(blocks)], axis=1).astype(F32)
    centred = x - jnp.mean(x, axis=1, keepdims=True)
    inv_std = lax.rsqrt(jnp.mean(centred * centred, axis=1, keepdims=True) + EPS)
    x_hat = centred * inv_std
    normed = x_hat.astype(BF16)
    queries = dot(normed, wq_v[...]).astype(BF16)
    keys = dot(normed, wk_v[...]).astype(BF16)
    values = dot(normed, wv_v[...]).astype(BF16)
    normed_t = jnp.transpose(normed)
    d_att = d_att_v[...]

    lane_head = iota((slots, width), 1) // HEAD_DIM

    def only(h, a):
        return jnp.where(lane_head == h, a, jnp.zeros_like(a))

    valid = iota((slots, slots), 1) < length
    attended = jnp.zeros((slots, width), F32)
    d_values = jnp.zeros((slots, width), F32)
    for h in range(heads):
        scores = dot(only(h, queries), keys, 1, 1) * scale + bias[h] + deg_terms[h]
        scores = jnp.where(valid, scores, -jnp.inf)
        exps = jnp.exp(scores - jnp.max(scores, axis=1, keepdims=True))
        probs = exps / jnp.sum(exps, axis=1, keepdims=True)
        probs_v[h] = probs
        probs_b = probs.astype(BF16)
        attended = attended + dot(probs_b, only(h, values))
        d_values = d_values + dot(probs_b, only(h, d_att), 0, 0)
    out_part = dot(attended.astype(BF16), cot_v[...], 0, 0).astype(BF16)
    for b in range(blocks):
        for k in range(2):
            grads[0, b // 2, 2 * (b % 2) + k] = out_part[
                k * quarter : (k + 1) * quarter, b * width : (b + 1) * width
            ]
    core_send(0)
    halves = (2, n_x, quarter, width)
    d_values = d_values.astype(BF16)
    grads[1] = dot(normed_t, d_values).astype(BF16).reshape(halves)
    core_send(1)

    d_queries = jnp.zeros((slots, width), F32)
    d_keys = jnp.zeros((slots, width), F32)
    for h in range(heads):
        probs = probs_v[h]
        d_probs = dot(only(h, d_att), values, 1, 1)
        ds = probs * (d_probs - jnp.sum(probs * d_probs, axis=1, keepdims=True))
        d_scores[h] = ds
        ds_b = ds.astype(BF16)
        d_queries = d_queries + dot(ds_b, only(h, keys))
        d_keys = d_keys + dot(ds_b, only(h, queries), 0, 0)
    d_queries = (d_queries * scale).astype(BF16)
    d_keys = (d_keys * scale).astype(BF16)
    x_far(0)
    x_far(1)
    grads[2] = dot(normed_t, d_keys).astype(BF16).reshape(halves)
    core_send(2)
    grads[3] = dot(normed_t, d_queries).astype(BF16).reshape(halves)
    core_send(3)

    d_normed = (
        dot(d_queries, wq_v[...], 1, 1)
        + dot(d_keys, wk_v[...], 1, 1)
        + dot(d_values, wv_v[...], 1, 1)
    )
    lead = jnp.where(me_n == 0, 1.0, 0.0)
    d_rows = lead * cot_v[...].astype(F32) + inv_std * (
        d_normed
        - jnp.mean(d_normed, axis=1, keepdims=True)
        - x_hat * jnp.mean(d_normed * x_hat, axis=1, keepdims=True)
    )
    for b in range(blocks):
        d_rows_v[b] = d_rows[:, b * width : (b + 1) * width].astype(BF16)
    for j in (2, 1, 3):
        p = lax.rem(me_n + j, n_node)
        remote(d_rows_v.at[p], y_in.at[me_n], fs.at[0], fr.at[0], node=p).start()
    y_in[me_n] = d_rows_v[me_n]

    def bucket_sums(h):
        def spd_block(i, totals):
            at = pl.ds(pl.multiple_of(i * step, step), step)
            bucket, ds = spd_v[at, :], d_scores[h, at, :]
            new = []
            for b in range(NSPD):
                kept = jnp.where(bucket == b, ds, 0.0)
                kept = kept[:, :128] + kept[:, 128:]
                new.append(totals[b] + (kept[0:8] + kept[8:16]) + (kept[16:24] + kept[24:32]))
            return tuple(new)

        totals = lax.fori_loop(
            0, slots // step, spd_block, tuple(jnp.zeros((8, 128), F32) for _ in range(NSPD))
        )
        sums[h * 128 : (h + 1) * 128, :] = jnp.zeros((128, 128), F32)
        for b in range(NSPD):
            at = h * 128 + b
            sums[at : at + 1, :] = jnp.sum(totals[b], axis=0, keepdims=True)
        by_key = jnp.sum(d_scores[h], axis=0, keepdims=True)
        kept = jnp.where(degree == iota((NDEG, slots), 0), by_key, 0.0)
        at = h * 128 + NSPD
        sums[at : at + NDEG, :] = kept[:, :128] + kept[:, 128:]

    x_far(2)
    x_far(3)
    for c in range(chunks):
        x_own(c)
    bucket_sums(0)
    for c in range(chunks):
        x_near(c)
    bucket_sums(1)
    for c in range(chunks):
        z_send(c)

    lists = jnp.where(iota((entries, slots), 0) == dest_v[...], 1.0, 0.0).astype(BF16)
    wait_bytes(y_in.at[pl.ds(0, n_node - 1)], fr.at[0])
    d_rows = y_in[0].astype(F32)
    for n in range(1, n_node):
        d_rows = d_rows + y_in[n].astype(F32)
    packed = dot(lists, d_rows.astype(BF16)).astype(BF16)
    left, right = packed[:, :half], packed[:, half:]
    shape = (n_batch, PAIR_ROWS, half)
    to_core[...] = jnp.where(me_r == 0, right, left).reshape(shape)
    remote(to_core, pack.at[me_r], fs.at[1], fr.at[1], replica=other).start()
    pack[me_r] = jnp.where(me_r == 0, left, right).reshape(shape)

    bucket_sums(2)
    z_back(0)
    z_back(1)
    bucket_sums(3)
    totals = dot(jnp.ones((8, 128), F32), sums[...], 1, 1, precision=lax.Precision.HIGHEST)
    small[...] = jnp.zeros_like(small)
    for h in range(heads):
        small[h : h + 1, :] = totals[0:1, h * 128 : (h + 1) * 128]
    remote(small, small_core, ts.at[0], tr.at[0], replica=other).start()
    z_back(2)
    z_back(3)
    wait_bytes(to_core, fr.at[1])
    for dx in (2, 1, 3, 0):
        first = lax.rem(me_x + dx, n_x) * n_z
        for dz in z_order + ((0,) if dx else ()):
            p = first + lax.rem(me_z + dz, n_z)
            remote(pack.at[:, p], table_in.at[:, me_b], fs.at[2], fr.at[2], batch=p).start()
    table_in[:, me_b] = pack[:, me_b]

    wait_bytes(reqs.at[0], gr.at[1])
    mine = iota((entries, 128), 1) == iota((entries, 128), 0) % PAIR_ROWS
    targets = []
    for r in range(2):
        for p in range(n_batch):
            spread[p * PAIR_ROWS : (p + 1) * PAIR_ROWS, :] = jnp.broadcast_to(
                reqs[r, p], (PAIR_ROWS, 128)
            )
        target = jnp.sum(jnp.where(mine, spread[...].astype(F32), 0.0), axis=1, keepdims=True) - 1.0
        flat = jnp.transpose(jnp.broadcast_to(target, (entries, 128)))[0:1, :].astype(I32)
        targets.append(flat)
    wait_bytes(small_core, tr.at[0])
    small_x[me_x] = small[...] + small_core[...]
    for to in (across_x, up, down):
        remote(
            small_x.at[me_x], small_x.at[me_x], ts.at[1], tr.at[1], batch=to * n_z + me_z
        ).start()

    for c in range(chunks):
        x_back(c)
    for c in range(chunks):
        core_back(c, me_x)
    row = iota((table_rows, entries), 0)
    for r in range(2):
        scatter[r] = jnp.where(row == targets[r], 1.0, 0.0).astype(BF16)
    for c in range(chunks):
        x_pass(c)
    wait_bytes(small_x.at[pl.ds(0, n_x - 1)], tr.at[1])
    total = small_x[0]
    for x in range(1, n_x):
        total = total + small_x[x]
    small_z[me_z] = total
    for j in z_order:
        p = lax.rem(me_z + j, n_z)
        remote(
            small_z.at[me_z], small_z.at[me_z], ts.at[2], tr.at[2], batch=me_x * n_z + p
        ).start()

    for c in range(chunks):
        x_done(c)
    wait_bytes(table_in.at[:, pl.ds(0, n_batch - 1)], fr.at[2])
    table_ref[...] = dot(scatter[0], table_in[0].reshape(entries, half)) + dot(
        scatter[1], table_in[1].reshape(entries, half)
    )
    writes = [pltpu.make_async_copy(table_ref, table_hbm_out, wsem.at[chunks])]
    writes[0].start()
    for c in range(chunks):
        x_last(c)
    wait_bytes(small_z.at[pl.ds(0, n_z - 1)], tr.at[2])
    total = small_z[0]
    for z in range(1, n_z):
        total = total + small_z[z]
    small_out[...] = total * (1.0 / copies)
    writes.append(pltpu.make_async_copy(small_out, small_hbm, wsem.at[chunks + 1]))
    writes[-1].start()
    for c in range(chunks):
        wait_bytes(out_ref.at[c, 0], rsem.at[5, c])
        writes.append(pltpu.make_async_copy(out_ref.at[c], out_hbm.at[c], wsem.at[c]))
        writes[-1].start()

    wait_bytes(ask.at[pl.ds(0, n_batch - 1)], gs.at[0])
    wait_bytes(reqs.at[0], gs.at[1])
    wait_bytes(rows_send.at[pl.ds(0, n_batch - 1)], gs.at[2])
    wait_bytes(rows.at[pl.ds(0, n_node - 1)], gs.at[3])
    wait_bytes(y_in.at[pl.ds(0, n_node - 1)], fs.at[0])
    wait_bytes(to_core, fs.at[1])
    wait_bytes(table_in.at[:, pl.ds(0, n_batch - 1)], fs.at[2])
    wait_bytes(small_core, ts.at[0])
    wait_bytes(small_x.at[pl.ds(0, n_x - 1)], ts.at[1])
    wait_bytes(small_z.at[pl.ds(0, n_z - 1)], ts.at[2])
    for c in range(chunks):
        wait_bytes(core_in.at[c], ssem.at[0, c])
        wait_bytes(x_far_in.at[c], ssem.at[1, c])
        wait_bytes(x_in.at[c], ssem.at[6, c])
        wait_bytes(z_in.at[c, pl.ds(0, n_z - 1)], ssem.at[2, c])
        wait_bytes(out_ref.at[c, 0, 0, pl.ds(0, n_z - 1)], ssem.at[3, c])
        wait_bytes(out_ref.at[c, 0, pl.ds(0, n_x - 1)], ssem.at[4, c])
        wait_bytes(out_ref.at[c, 0], ssem.at[5, c])
    for write in writes:
        write.wait()


def finish_kernel(
    sums_hbm,
    table_hbm,
    small_hbm,
    table_out,
    query_out,
    key_out,
    value_out,
    out_out,
    spd_out,
    deg_out,
    sums_v,
    small_v,
    table_v,
    wide,
    outer,
    rsem,
    wsem,
):
    chunks = sums_v.shape[0]
    width = outer.shape[0]
    reads = [
        pltpu.make_async_copy(sums_hbm.at[c], sums_v.at[c], rsem.at[c]) for c in range(chunks)
    ]
    reads.append(pltpu.make_async_copy(small_hbm, small_v, rsem.at[chunks]))
    reads.append(pltpu.make_async_copy(table_hbm, table_v, rsem.at[chunks + 1]))
    for read in reads:
        read.start()
    reads[0].wait()
    step = 64
    steps = width // step

    def widen_outer(i, carry):
        at = pl.ds(pl.multiple_of(i * step, step), step)
        for b in range(outer.shape[1] // width):
            row = pl.ds(pl.multiple_of(i * step + b * width, step), step)
            outer[at, b * width : (b + 1) * width] = sums_v[0, row].astype(F32)
        return carry

    lax.fori_loop(0, steps, widen_outer, 0)
    writes = [pltpu.make_async_copy(outer, out_out, wsem.at[0])]
    writes[0].start()
    for c, out in ((1, value_out), (2, key_out), (3, query_out)):
        reads[c].wait()

        def widen(i, carry, c=c):
            at = pl.ds(pl.multiple_of(i * width, width), width)
            wide[c - 1, at] = sums_v[c, at].astype(F32)
            return carry

        lax.fori_loop(0, sums_v.shape[1] // width, widen, 0)
        writes.append(pltpu.make_async_copy(wide.at[c - 1], out, wsem.at[c]))
        writes[-1].start()
    reads[chunks + 1].wait()
    writes.append(pltpu.make_async_copy(table_v, table_out, wsem.at[chunks]))
    writes[-1].start()
    reads[chunks].wait()
    heads = spd_out.shape[0]
    spd_out[...] = small_v[0:heads, 0:NSPD]
    deg_out[...] = small_v[0:heads, NSPD : NSPD + NDEG]
    for write in writes:
        write.wait()


def on_device(
    embed_table,
    owner_shard,
    local_row,
    lengths,
    spd_bucket,
    degree_bucket,
    w_query,
    w_key,
    w_value,
    w_out,
    spd_bias,
    degree_bias,
    cotangent,
):
    n_batch, n_node = lax.axis_size("batch"), lax.axis_size("node")
    n_z = Z_SIZE
    n_x = n_batch // n_z
    _, slots, feature_dim = cotangent.shape
    table_rows = embed_table.shape[0]
    width = feature_dim // n_node
    half = width // 2
    heads = width // HEAD_DIM
    entries = n_batch * PAIR_ROWS
    chunks = 4
    quarter = feature_dim // (2 * n_x)
    piece = quarter // n_z
    vmem = pl.BlockSpec(memory_space=pltpu.VMEM)
    smem = pl.BlockSpec(memory_space=pltpu.SMEM)
    hbm = pl.BlockSpec(memory_space=pltpu.HBM)
    shaped = jax.ShapeDtypeStruct
    dma = pltpu.SemaphoreType.DMA
    v = pltpu.VMEM

    sums, table_grad, small = pl.pallas_call(
        functools.partial(train_kernel, n_batch, n_node),
        out_shape=(
            shaped((chunks, 2, n_x, n_z, piece, width), BF16),
            shaped((table_rows, half), F32),
            shaped((8, 128), F32),
        ),
        in_specs=[smem] * 2 + [hbm] * 11,
        out_specs=(hbm, hbm, hbm),
        scratch_shapes=[
            v((1, 1), I32),
            v((1, slots), I32),
            v((1, slots), I32),
            v((1, slots), I32),
            v((table_rows, width), BF16),
            v((slots, slots), I32),
            v((slots, feature_dim), BF16),
            v((width, feature_dim), BF16),
            v((feature_dim, width), BF16),
            v((feature_dim, width), BF16),
            v((feature_dim, width), BF16),
            v((n_batch, 1, 128), I32),
            v((2, n_batch, 1, 128), I32),
            v((entries, 128), I32),
            v((n_batch, PAIR_ROWS, width), BF16),
            v((n_batch, PAIR_ROWS, width), BF16),
            v((n_node, slots, width), BF16),
            v((1, slots), I32),
            v((heads, slots, slots), F32),
            v((slots, width), BF16),
            v((heads, slots, slots), F32),
            v((heads, slots, slots), F32),
            v((heads * 128, 128), F32),
            v((8, 128), F32),
            v((chunks, 2, n_x, quarter, width), BF16),
            v((n_node, slots, width), BF16),
            v((chunks, n_x, quarter, width), BF16),
            v((chunks, n_x, quarter, width), BF16),
            v((chunks, 2, quarter // 2, width), BF16),
            v((chunks, 2, quarter, width), BF16),
            v((chunks, n_z, piece, width), BF16),
            v((chunks, n_z, piece, width), BF16),
            v((n_node, slots, width), BF16),
            v((2, n_batch, PAIR_ROWS, half), BF16),
            v((n_batch, PAIR_ROWS, half), BF16),
            v((2, n_batch, PAIR_ROWS, half), BF16),
            v((8, 128), F32),
            v((n_x, 8, 128), F32),
            v((n_z, 8, 128), F32),
            v((2, table_rows, entries), BF16),
            v((chunks, 2, n_x, n_z, piece, width), BF16),
            v((table_rows, half), F32),
            v((8, 128), F32),
            dma((11,)),
            dma((4,)),
            dma((4,)),
            dma((7, chunks)),
            dma((7, chunks)),
            dma((5, chunks)),
            dma((3,)),
            dma((3,)),
            dma((3,)),
            dma((3,)),
            dma((chunks + 2,)),
        ],
        compiler_params=pltpu.CompilerParams(
            collective_id=0, has_side_effects=True, vmem_limit_bytes=61 * 2**20
        ),
        name="layer_and_exchanges",
    )(
        spd_bias.T,
        degree_bias.T,
        lengths.reshape(1, 1),
        owner_shard.reshape(1, slots),
        local_row,
        degree_bucket,
        embed_table,
        spd_bucket.reshape(slots, slots),
        cotangent.reshape(slots, feature_dim),
        w_out,
        w_query,
        w_key,
        w_value,
    )

    square = shaped((feature_dim, width), F32)
    table_grad, query_grad, key_grad, value_grad, out_grad, spd_grad, degree_grad = pl.pallas_call(
        finish_kernel,
        out_shape=(
            shaped((table_rows, half), F32),
            square,
            square,
            square,
            shaped((width, feature_dim), F32),
            shaped((heads, NSPD), F32),
            shaped((heads, NDEG), F32),
        ),
        in_specs=[hbm] * 3,
        out_specs=(hbm,) * 5 + (vmem, vmem),
        scratch_shapes=[
            v((chunks, feature_dim, width), BF16),
            v((8, 128), F32),
            v((table_rows, half), F32),
            v((3, feature_dim, width), F32),
            v((width, feature_dim), F32),
            dma((chunks + 2,)),
            dma((chunks + 1,)),
        ],
        compiler_params=pltpu.CompilerParams(vmem_limit_bytes=61 * 2**20),
        name="write_outputs",
    )(sums.reshape(chunks, feature_dim, width), table_grad, small)
    return table_grad, query_grad, key_grad, value_grad, out_grad, spd_grad.T, degree_grad.T


def solution(mesh):
    placed = (
        P("batch", None),
        P(("batch", "replica"), None, None),
        P(("batch", "replica"), None),
        P(("batch", "replica")),
        P(("batch", "replica"), None, None),
        P(("batch", "replica"), None),
        P(None, "node"),
        P(None, "node"),
        P(None, "node"),
        P("node", None),
        P(None, "node"),
        P(None, "node"),
        P(("batch", "replica"), None, None),
    )
    return jax.shard_map(
        on_device,
        mesh=mesh,
        in_specs=placed,
        out_specs=(
            P("batch", ("node", "replica")),
            P(None, "node"),
            P(None, "node"),
            P(None, "node"),
            P("node", None),
            P(None, "node"),
            P(None, "node"),
        ),
        check_vma=False,
    )
```

```python
import functools

import jax
import jax.numpy as jnp
from jax import lax
from jax.experimental import pallas as pl
from jax.experimental.pallas import tpu as pltpu
from jax.sharding import PartitionSpec as P

HEAD_DIM = 64
NSPD = 16
NDEG = 32
EPS = 1e-05
PAIR_ROWS = 16
Z_SIZE = 8
MESH = pl.DeviceIdType.MESH
F32 = jnp.float32
BF16 = jnp.bfloat16
I32 = jnp.int32


def iota(shape, dim):
    return lax.broadcasted_iota(I32, shape, dim)


def dot(a, b, ca=1, cb=0, precision=None):
    return lax.dot_general(
        a, b, (((ca,), (cb,)), ((), ())), preferred_element_type=F32, precision=precision
    )


def remote(src, dst, send_sem, recv_sem, **where):
    return pltpu.make_async_remote_copy(
        src_ref=src,
        dst_ref=dst,
        send_sem=send_sem,
        recv_sem=recv_sem,
        device_id=where,
        device_id_type=MESH,
    )


def wait_bytes(ref, sem):
    pltpu.make_async_copy(ref, ref, sem).wait()


def train_kernel(
    n_batch,
    n_node,
    spd_bias_ref,
    deg_bias_ref,
    length_hbm,
    owner_hbm,
    local_hbm,
    deg_hbm,
    table_hbm,
    spd_hbm,
    cot_hbm,
    wo_hbm,
    wq_hbm,
    wk_hbm,
    wv_hbm,
    out_hbm,
    table_hbm_out,
    small_hbm,
    length_ref,
    owner_v,
    local_v,
    deg_v,
    table_v,
    spd_v,
    cot_v,
    wo_v,
    wq_v,
    wk_v,
    wv_v,
    ask,
    reqs,
    spread,
    rows_send,
    rows_recv,
    rows,
    dest_v,
    bias,
    d_att_v,
    probs_v,
    d_scores,
    sums,
    small,
    grads,
    d_rows_v,
    core_in,
    core_sum,
    x_far_in,
    x_in,
    x_sum,
    z_in,
    y_in,
    pack,
    to_core,
    table_in,
    small_core,
    small_x,
    small_z,
    scatter,
    lists,
    out_ref,
    table_ref,
    small_out,
    lsem,
    gs,
    gr,
    ssem,
    rsem,
    xsem,
    fs,
    fr,
    ts,
    tr,
    wsem,
):
    me_b, me_n, me_r = lax.axis_index("batch"), lax.axis_index("node"), lax.axis_index("replica")
    n_z = Z_SIZE
    n_x = n_batch // n_z
    me_x, me_z = me_b // n_z, me_b % n_z
    other = 1 - me_r
    up, down, across_x = lax.rem(me_x + 1, n_x), lax.rem(me_x + 3, n_x), lax.rem(me_x + 2, n_x)
    slots, feature_dim = cot_v.shape
    table_rows, width = table_v.shape
    heads = width // HEAD_DIM
    blocks = feature_dim // width
    half = width // 2
    entries = n_batch * PAIR_ROWS
    chunks = out_ref.shape[0]
    piece = out_ref.shape[4]
    quarter = n_z * piece
    copies = 2.0 * n_batch
    scale = HEAD_DIM ** (-0.5)
    step = 32
    z_order = (4, 3, 5, 2, 6, 1, 7)
    barrier = pltpu.get_barrier_semaphore()

    def signal_batch(j, carry):
        p = lax.rem(me_b + j, n_batch)
        pl.semaphore_signal(barrier, inc=1, device_id={"batch": p}, device_id_type=MESH)
        return carry

    lax.fori_loop(1, n_batch, signal_batch, 0)
    for j in range(1, n_node):
        p = lax.rem(me_n + j, n_node)
        pl.semaphore_signal(barrier, inc=1, device_id={"node": p}, device_id_type=MESH)
    pl.semaphore_signal(barrier, inc=1, device_id={"replica": other}, device_id_type=MESH)

    columns = pl.ds(pl.multiple_of(me_n * width, width), width)
    loads = [
        pltpu.make_async_copy(src, dst, lsem.at[i])
        for i, (src, dst) in enumerate(
            (
                (owner_hbm, owner_v),
                (local_hbm, local_v),
                (deg_hbm, deg_v),
                (spd_hbm, spd_v),
                (table_hbm.at[:, columns], table_v),
                (cot_hbm, cot_v),
                (wo_hbm, wo_v),
                (wq_hbm, wq_v),
                (wk_hbm, wk_v),
                (wv_hbm, wv_v),
                (length_hbm, length_ref),
            )
        )
    ]
    for load in loads:
        load.start()

    loads[0].wait()
    loads[1].wait()
    owner_row = owner_v[...]
    across = jnp.broadcast_to(owner_row, (slots, slots))
    owner_down = jnp.transpose(across)
    same = across == owner_down
    r0, r1 = iota((slots, slots), 0), iota((slots, slots), 1)
    rank_row = jnp.sum(jnp.where(same & (r0 < r1), 1.0, 0.0), axis=0, keepdims=True).astype(I32)
    rank_col = jnp.sum(jnp.where(same & (r1 < r0), 1.0, 0.0), axis=1, keepdims=True).astype(I32)
    dest_v[...] = owner_row * PAIR_ROWS + rank_row
    dest_col = owner_down[:, 0:1] * PAIR_ROWS + rank_col

    wanted = local_v[...] + 1
    hit = owner_row == iota((n_batch, slots), 0)
    high = jnp.where(hit, (wanted // 32).astype(F32), 0.0).astype(BF16)
    low = jnp.where(hit, (wanted % 32).astype(F32), 0.0).astype(BF16)
    at_rank = jnp.where(rank_col == iota((slots, 128), 1), 1.0, 0.0).astype(BF16)
    listed = (dot(high, at_rank) * 32.0 + dot(low, at_rank)).astype(I32)
    for o in range(n_batch):
        ask[o] = listed[o : o + 1, :]

    pl.semaphore_wait(barrier, n_batch - 1 + n_node - 1 + 1)

    def send_ask(j, carry):
        p = lax.rem(me_b + j, n_batch)
        remote(ask.at[p], reqs.at[me_r, me_b], gs.at[0], gr.at[0], batch=p).start()
        return carry

    lax.fori_loop(1, n_batch, send_ask, 0)
    reqs[me_r, me_b] = ask[me_b]

    loads[2].wait()
    loads[3].wait()

    def bias_block(i, carry):
        at = pl.ds(pl.multiple_of(i * step, step), step)
        bucket = spd_v[at, :]
        terms = [jnp.full(bucket.shape, spd_bias_ref[h, 0], F32) for h in range(heads)]
        for b in range(1, NSPD):
            is_b = bucket == b
            terms = [jnp.where(is_b, spd_bias_ref[h, b], terms[h]) for h in range(heads)]
        for h in range(heads):
            bias[h, at, :] = terms[h]
        return carry

    lax.fori_loop(0, slots // step, bias_block, 0)
    place = jnp.where(iota((slots, entries), 1) == dest_col, 1.0, 0.0).astype(BF16)

    loads[4].wait()
    wait_bytes(ask.at[pl.ds(0, n_batch - 1)], gr.at[0])
    remote(reqs.at[me_r], reqs.at[me_r], gs.at[1], gr.at[1], replica=other).start()
    group = n_z * PAIR_ROWS
    mine = iota((group, 128), 1) == iota((group, 128), 0) % PAIR_ROWS
    for dx in (2, 1, 3, 0):
        first = lax.rem(me_x + dx, n_x) * n_z
        for k in range(n_z):
            spread[k * PAIR_ROWS : (k + 1) * PAIR_ROWS, :] = jnp.broadcast_to(
                reqs[me_r, first + k], (PAIR_ROWS, 128)
            )
        listed = spread[0:group, :].astype(F32)
        target = jnp.sum(jnp.where(mine, listed, 0.0), axis=1, keepdims=True).astype(I32) - 1
        pick = jnp.where(iota((group, table_rows), 1) == target, 1.0, 0.0).astype(BF16)
        rows_send[pl.ds(first, n_z)] = (
            dot(pick, table_v[...]).astype(BF16).reshape(n_z, PAIR_ROWS, width)
        )
        for dz in z_order + ((0,) if dx else ()):
            p = first + lax.rem(me_z + dz, n_z)
            remote(rows_send.at[p], rows_recv.at[me_b], gs.at[2], gr.at[2], batch=p).start()
    rows_recv[me_b] = rows_send[me_b]

    loads[5].wait()
    loads[6].wait()
    loads[10].wait()
    length = length_ref[...]
    d_masked = jnp.where(
        iota((slots, feature_dim), 0) < length, cot_v[...].astype(F32), 0.0
    ).astype(BF16)
    cot_v[...] = d_masked
    d_att_v[...] = dot(d_masked, wo_v[...], 1, 1).astype(BF16)
    degree = deg_v[...]
    deg_terms = []
    for h in range(heads):
        term = jnp.full(degree.shape, deg_bias_ref[h, 0], F32)
        for b in range(1, NDEG):
            term = jnp.where(degree == b, deg_bias_ref[h, b], term)
        deg_terms.append(term)

    wait_bytes(rows_recv.at[pl.ds(0, n_batch - 1)], gr.at[2])
    rows[me_n] = dot(place, rows_recv[...].reshape(entries, width)).astype(BF16)
    for j in (2, 1, 3):
        p = lax.rem(me_n + j, n_node)
        remote(rows.at[me_n], rows.at[me_n], gs.at[3], gr.at[3], node=p).start()
    wait_bytes(reqs.at[0], gr.at[1])
    mine = iota((entries, 128), 1) == iota((entries, 128), 0) % PAIR_ROWS
    targets = []
    for r in range(2):
        for p in range(n_batch):
            spread[p * PAIR_ROWS : (p + 1) * PAIR_ROWS, :] = jnp.broadcast_to(
                reqs[r, p], (PAIR_ROWS, 128)
            )
        target = jnp.sum(jnp.where(mine, spread[...].astype(F32), 0.0), axis=1, keepdims=True) - 1.0
        flat = jnp.transpose(jnp.broadcast_to(target, (entries, 128)))[0:1, :].astype(I32)
        targets.append(flat)
    row = iota((table_rows, entries), 0)
    for r in range(2):
        scatter[r] = jnp.where(row == targets[r], 1.0, 0.0).astype(BF16)
    lists[...] = jnp.where(iota((entries, slots), 0) == dest_v[...], 1.0, 0.0).astype(BF16)
    for load in loads[7:10]:
        load.wait()
    wait_bytes(rows.at[pl.ds(0, n_node - 1)], gr.at[3])

    def core_send(c):
        remote(grads.at[c, other], core_in.at[c], ssem.at[0, c], rsem.at[0, c], replica=other).start()

    first_half, last_half = pl.ds(0, quarter // 2), pl.ds(quarter // 2, quarter // 2)

    straight = (0, 1)

    def x_far(c):
        wait_bytes(core_in.at[c], rsem.at[0, c])
        core_sum[c] = (grads[c, me_r].astype(F32) + core_in[c].astype(F32)).astype(BF16)
        for d, (to, part) in enumerate(((up, first_half), (down, last_half))):
            remote(
                core_sum.at[c, across_x, part],
                x_far_in.at[c, d],
                ssem.at[1, c],
                rsem.at[1, c],
                batch=(across_x if c in straight else to) * n_z + me_z,
            ).start()

    def x_share(c, d, to, part):
        remote(
            core_sum.at[c, to, part],
            x_in.at[c, d, part],
            ssem.at[6, c],
            rsem.at[6, c],
            batch=to * n_z + me_z,
        ).start()

    def x_own(c):
        x_share(c, 0, up, last_half)
        x_share(c, 1, down, first_half)
        if c in straight:
            x_share(c, 0, up, first_half)
            x_share(c, 1, down, last_half)

    def x_near(c):
        if c in straight:
            return
        wait_bytes(x_far_in.at[c], rsem.at[1, c])
        for d, (to, part) in enumerate(((up, first_half), (down, last_half))):
            core_sum[c, to, part] = (
                core_sum[c, to, part].astype(F32) + x_far_in[c, d].astype(F32)
            ).astype(BF16)
            x_share(c, d, to, part)

    def z_send(c):
        wait_bytes(x_in.at[c], rsem.at[6, c])
        total = core_sum[c, me_x].astype(F32) + x_in[c, 0].astype(F32) + x_in[c, 1].astype(F32)
        if c in straight:
            wait_bytes(x_far_in.at[c], rsem.at[1, c])
            total = total + x_far_in[c].astype(F32).reshape(quarter, width)
        x_sum[c] = total.astype(BF16).reshape(n_z, piece, width)
        for j in z_order:
            p = lax.rem(me_z + j, n_z)
            remote(
                x_sum.at[c, p],
                z_in.at[c, me_z],
                ssem.at[2, c],
                rsem.at[2, c],
                batch=me_x * n_z + p,
            ).start()
        z_in[c, me_z] = x_sum[c, me_z]

    def z_back(c):
        wait_bytes(z_in.at[c, pl.ds(0, n_z - 1)], rsem.at[2, c])
        total = z_in[c, 0].astype(F32)
        for z in range(1, n_z):
            total = total + z_in[c, z].astype(F32)
        out_ref[c, me_r, me_x, me_z] = (total * (1.0 / copies)).astype(BF16)
        done = out_ref.at[c, me_r, me_x, me_z]
        for j in z_order:
            p = lax.rem(me_z + j, n_z)
            remote(done, done, ssem.at[3, c], rsem.at[3, c], batch=me_x * n_z + p).start()

    def core_back(c, x):
        done = out_ref.at[c, me_r, x]
        remote(done, done, ssem.at[5, c], rsem.at[5, c], replica=other).start()

    low, high = pl.ds(0, n_z // 2), pl.ds(n_z // 2, n_z // 2)

    def x_give(c, k, source, part, to):
        done = out_ref.at[c, me_r, source, part]
        remote(done, done, ssem.at[4, c], xsem.at[k, c], batch=to * n_z + me_z).start()

    def x_back(c):
        wait_bytes(out_ref.at[c, 0, 0, pl.ds(0, n_z - 1)], rsem.at[3, c])
        x_give(c, 0, me_x, low, up)
        x_give(c, 1, me_x, high, down)
        x_give(c, 2, me_x, high, up)
        x_give(c, 3, me_x, low, down)

    def x_pass(c):
        wait_bytes(out_ref.at[c, 0, 0, low], xsem.at[0, c])
        x_give(c, 4, down, low, up)
        wait_bytes(out_ref.at[c, 0, 0, low], xsem.at[1, c])
        x_give(c, 4, up, high, down)

    def x_done(c):
        wait_bytes(out_ref.at[c, 0, 0, low], xsem.at[2, c])
        core_back(c, down)
        wait_bytes(out_ref.at[c, 0, 0, low], xsem.at[3, c])
        core_back(c, up)

    def x_last(c):
        wait_bytes(out_ref.at[c, 0, 0], xsem.at[4, c])
        core_back(c, across_x)

    x = jnp.concatenate([rows[b] for b in range(blocks)], axis=1).astype(F32)
    centred = x - jnp.mean(x, axis=1, keepdims=True)
    inv_std = lax.rsqrt(jnp.mean(centred * centred, axis=1, keepdims=True) + EPS)
    x_hat = centred * inv_std
    normed = x_hat.astype(BF16)
    queries = dot(normed, wq_v[...]).astype(BF16)
    keys = dot(normed, wk_v[...]).astype(BF16)
    values = dot(normed, wv_v[...]).astype(BF16)
    normed_t = jnp.transpose(normed)
    d_att = d_att_v[...]

    lane_head = iota((slots, width), 1) // HEAD_DIM

    def only(h, a):
        return jnp.where(lane_head == h, a, jnp.zeros_like(a))

    valid = iota((slots, slots), 1) < length
    attended = jnp.zeros((slots, width), F32)
    d_values = jnp.zeros((slots, width), F32)
    for h in range(heads):
        scores = dot(only(h, queries), keys, 1, 1) * scale + bias[h] + deg_terms[h]
        scores = jnp.where(valid, scores, -jnp.inf)
        exps = jnp.exp(scores - jnp.max(scores, axis=1, keepdims=True))
        probs = exps / jnp.sum(exps, axis=1, keepdims=True)
        probs_v[h] = probs
        probs_b = probs.astype(BF16)
        attended = attended + dot(probs_b, only(h, values))
        d_values = d_values + dot(probs_b, only(h, d_att), 0, 0)
    out_part = dot(attended.astype(BF16), cot_v[...], 0, 0).astype(BF16)
    for b in range(blocks):
        for k in range(2):
            grads[0, b // 2, 2 * (b % 2) + k] = out_part[
                k * quarter : (k + 1) * quarter, b * width : (b + 1) * width
            ]
    core_send(0)
    halves = (2, n_x, quarter, width)
    d_values = d_values.astype(BF16)
    grads[1] = dot(normed_t, d_values).astype(BF16).reshape(halves)
    core_send(1)

    d_queries = jnp.zeros((slots, width), F32)
    d_keys = jnp.zeros((slots, width), F32)
    for h in range(heads):
        probs = probs_v[h]
        d_probs = dot(only(h, d_att), values, 1, 1)
        ds = probs * (d_probs - jnp.sum(probs * d_probs, axis=1, keepdims=True))
        d_scores[h] = ds
        ds_b = ds.astype(BF16)
        d_queries = d_queries + dot(ds_b, only(h, keys))
        d_keys = d_keys + dot(ds_b, only(h, queries), 0, 0)
    d_queries = (d_queries * scale).astype(BF16)
    d_keys = (d_keys * scale).astype(BF16)
    x_far(0)
    x_far(1)
    grads[2] = dot(normed_t, d_keys).astype(BF16).reshape(halves)
    core_send(2)
    grads[3] = dot(normed_t, d_queries).astype(BF16).reshape(halves)
    core_send(3)

    d_normed = (
        dot(d_queries, wq_v[...], 1, 1)
        + dot(d_keys, wk_v[...], 1, 1)
        + dot(d_values, wv_v[...], 1, 1)
    )
    lead = jnp.where(me_n == 0, 1.0, 0.0)
    d_rows = lead * cot_v[...].astype(F32) + inv_std * (
        d_normed
        - jnp.mean(d_normed, axis=1, keepdims=True)
        - x_hat * jnp.mean(d_normed * x_hat, axis=1, keepdims=True)
    )
    for b in range(blocks):
        d_rows_v[b] = d_rows[:, b * width : (b + 1) * width].astype(BF16)
    for j in (2, 1, 3):
        p = lax.rem(me_n + j, n_node)
        remote(d_rows_v.at[p], y_in.at[me_n], fs.at[0], fr.at[0], node=p).start()
    y_in[me_n] = d_rows_v[me_n]

    def bucket_sums(h):
        def spd_block(i, totals):
            at = pl.ds(pl.multiple_of(i * step, step), step)
            bucket, ds = spd_v[at, :], d_scores[h, at, :]
            new = []
            for b in range(NSPD):
                kept = jnp.where(bucket == b, ds, 0.0)
                kept = kept[:, :128] + kept[:, 128:]
                new.append(totals[b] + (kept[0:8] + kept[8:16]) + (kept[16:24] + kept[24:32]))
            return tuple(new)

        totals = lax.fori_loop(
            0, slots // step, spd_block, tuple(jnp.zeros((8, 128), F32) for _ in range(NSPD))
        )
        sums[h * 128 : (h + 1) * 128, :] = jnp.zeros((128, 128), F32)
        for b in range(NSPD):
            at = h * 128 + b
            sums[at : at + 1, :] = jnp.sum(totals[b], axis=0, keepdims=True)
        by_key = jnp.sum(d_scores[h], axis=0, keepdims=True)
        kept = jnp.where(degree == iota((NDEG, slots), 0), by_key, 0.0)
        at = h * 128 + NSPD
        sums[at : at + NDEG, :] = kept[:, :128] + kept[:, 128:]

    x_far(2)
    x_far(3)
    for c in range(chunks):
        x_own(c)
    bucket_sums(0)
    for c in range(chunks):
        x_near(c)
    bucket_sums(1)
    for c in range(chunks):
        z_send(c)

    wait_bytes(y_in.at[pl.ds(0, n_node - 1)], fr.at[0])
    d_rows = y_in[0].astype(F32)
    for n in range(1, n_node):
        d_rows = d_rows + y_in[n].astype(F32)
    packed = dot(lists[...], d_rows.astype(BF16)).astype(BF16)
    left, right = packed[:, :half], packed[:, half:]
    shape = (n_batch, PAIR_ROWS, half)
    to_core[...] = jnp.where(me_r == 0, right, left).reshape(shape)
    remote(to_core, pack.at[me_r], fs.at[1], fr.at[1], replica=other).start()
    pack[me_r] = jnp.where(me_r == 0, left, right).reshape(shape)

    bucket_sums(2)
    z_back(0)
    z_back(1)
    bucket_sums(3)
    totals = dot(jnp.ones((8, 128), F32), sums[...], 1, 1, precision=lax.Precision.HIGHEST)
    small[...] = jnp.zeros_like(small)
    for h in range(heads):
        small[h : h + 1, :] = totals[0:1, h * 128 : (h + 1) * 128]
    remote(small, small_core, ts.at[0], tr.at[0], replica=other).start()
    z_back(2)
    z_back(3)
    wait_bytes(to_core, fr.at[1])
    for dx in (2, 1, 3, 0):
        first = lax.rem(me_x + dx, n_x) * n_z
        for dz in z_order + ((0,) if dx else ()):
            p = first + lax.rem(me_z + dz, n_z)
            remote(pack.at[:, p], table_in.at[:, me_b], fs.at[2], fr.at[2], batch=p).start()
    table_in[:, me_b] = pack[:, me_b]

    wait_bytes(small_core, tr.at[0])
    small_x[me_x] = small[...] + small_core[...]
    for to in (across_x, up, down):
        remote(
            small_x.at[me_x], small_x.at[me_x], ts.at[1], tr.at[1], batch=to * n_z + me_z
        ).start()

    for c in range(chunks):
        x_back(c)
    for c in range(chunks):
        core_back(c, me_x)
    for c in range(chunks):
        x_pass(c)
    wait_bytes(small_x.at[pl.ds(0, n_x - 1)], tr.at[1])
    total = small_x[0]
    for x in range(1, n_x):
        total = total + small_x[x]
    small_z[me_z] = total
    for j in z_order:
        p = lax.rem(me_z + j, n_z)
        remote(
            small_z.at[me_z], small_z.at[me_z], ts.at[2], tr.at[2], batch=me_x * n_z + p
        ).start()

    for c in range(chunks):
        x_done(c)
    wait_bytes(table_in.at[:, pl.ds(0, n_batch - 1)], fr.at[2])
    table_ref[...] = dot(scatter[0], table_in[0].reshape(entries, half)) + dot(
        scatter[1], table_in[1].reshape(entries, half)
    )
    writes = [pltpu.make_async_copy(table_ref, table_hbm_out, wsem.at[chunks])]
    writes[0].start()
    for c in range(chunks):
        x_last(c)
    wait_bytes(small_z.at[pl.ds(0, n_z - 1)], tr.at[2])
    total = small_z[0]
    for z in range(1, n_z):
        total = total + small_z[z]
    small_out[...] = total * (1.0 / copies)
    writes.append(pltpu.make_async_copy(small_out, small_hbm, wsem.at[chunks + 1]))
    writes[-1].start()
    for c in range(chunks):
        wait_bytes(out_ref.at[c, 0], rsem.at[5, c])
        writes.append(pltpu.make_async_copy(out_ref.at[c], out_hbm.at[c], wsem.at[c]))
        writes[-1].start()

    wait_bytes(ask.at[pl.ds(0, n_batch - 1)], gs.at[0])
    wait_bytes(reqs.at[0], gs.at[1])
    wait_bytes(rows_send.at[pl.ds(0, n_batch - 1)], gs.at[2])
    wait_bytes(rows.at[pl.ds(0, n_node - 1)], gs.at[3])
    wait_bytes(y_in.at[pl.ds(0, n_node - 1)], fs.at[0])
    wait_bytes(to_core, fs.at[1])
    wait_bytes(table_in.at[:, pl.ds(0, n_batch - 1)], fs.at[2])
    wait_bytes(small_core, ts.at[0])
    wait_bytes(small_x.at[pl.ds(0, n_x - 1)], ts.at[1])
    wait_bytes(small_z.at[pl.ds(0, n_z - 1)], ts.at[2])
    for c in range(chunks):
        wait_bytes(core_in.at[c], ssem.at[0, c])
        wait_bytes(x_far_in.at[c], ssem.at[1, c])
        wait_bytes(x_in.at[c], ssem.at[6, c])
        wait_bytes(z_in.at[c, pl.ds(0, n_z - 1)], ssem.at[2, c])
        wait_bytes(out_ref.at[c, 0, 0, pl.ds(0, n_z - 1)], ssem.at[3, c])
        wait_bytes(out_ref.at[c, 0, pl.ds(0, n_x - 1)], ssem.at[4, c])
        wait_bytes(out_ref.at[c, 0], ssem.at[5, c])
    for write in writes:
        write.wait()


def finish_kernel(
    sums_hbm,
    table_hbm,
    small_hbm,
    table_out,
    query_out,
    key_out,
    value_out,
    out_out,
    spd_out,
    deg_out,
    sums_v,
    small_v,
    table_v,
    wide,
    outer,
    rsem,
    wsem,
):
    chunks = sums_v.shape[0]
    width = outer.shape[0]
    reads = [
        pltpu.make_async_copy(sums_hbm.at[c], sums_v.at[c], rsem.at[c]) for c in range(chunks)
    ]
    reads.append(pltpu.make_async_copy(small_hbm, small_v, rsem.at[chunks]))
    reads.append(pltpu.make_async_copy(table_hbm, table_v, rsem.at[chunks + 1]))
    for read in reads:
        read.start()
    reads[0].wait()
    step = 64
    steps = width // step

    def widen_outer(i, carry):
        at = pl.ds(pl.multiple_of(i * step, step), step)
        for b in range(outer.shape[1] // width):
            row = pl.ds(pl.multiple_of(i * step + b * width, step), step)
            outer[at, b * width : (b + 1) * width] = sums_v[0, row].astype(F32)
        return carry

    lax.fori_loop(0, steps, widen_outer, 0)
    writes = [pltpu.make_async_copy(outer, out_out, wsem.at[0])]
    writes[0].start()
    for c, out in ((1, value_out), (2, key_out), (3, query_out)):
        reads[c].wait()

        def widen(i, carry, c=c):
            at = pl.ds(pl.multiple_of(i * width, width), width)
            wide[c - 1, at] = sums_v[c, at].astype(F32)
            return carry

        lax.fori_loop(0, sums_v.shape[1] // width, widen, 0)
        writes.append(pltpu.make_async_copy(wide.at[c - 1], out, wsem.at[c]))
        writes[-1].start()
    reads[chunks + 1].wait()
    writes.append(pltpu.make_async_copy(table_v, table_out, wsem.at[chunks]))
    writes[-1].start()
    reads[chunks].wait()
    heads = spd_out.shape[0]
    spd_out[...] = small_v[0:heads, 0:NSPD]
    deg_out[...] = small_v[0:heads, NSPD : NSPD + NDEG]
    for write in writes:
        write.wait()


def on_device(
    embed_table,
    owner_shard,
    local_row,
    lengths,
    spd_bucket,
    degree_bucket,
    w_query,
    w_key,
    w_value,
    w_out,
    spd_bias,
    degree_bias,
    cotangent,
):
    n_batch, n_node = lax.axis_size("batch"), lax.axis_size("node")
    n_z = Z_SIZE
    n_x = n_batch // n_z
    _, slots, feature_dim = cotangent.shape
    table_rows = embed_table.shape[0]
    width = feature_dim // n_node
    half = width // 2
    heads = width // HEAD_DIM
    entries = n_batch * PAIR_ROWS
    chunks = 4
    quarter = feature_dim // (2 * n_x)
    piece = quarter // n_z
    vmem = pl.BlockSpec(memory_space=pltpu.VMEM)
    smem = pl.BlockSpec(memory_space=pltpu.SMEM)
    hbm = pl.BlockSpec(memory_space=pltpu.HBM)
    shaped = jax.ShapeDtypeStruct
    dma = pltpu.SemaphoreType.DMA
    v = pltpu.VMEM

    sums, table_grad, small = pl.pallas_call(
        functools.partial(train_kernel, n_batch, n_node),
        out_shape=(
            shaped((chunks, 2, n_x, n_z, piece, width), BF16),
            shaped((table_rows, half), F32),
            shaped((8, 128), F32),
        ),
        in_specs=[smem] * 2 + [hbm] * 11,
        out_specs=(hbm, hbm, hbm),
        scratch_shapes=[
            v((1, 1), I32),
            v((1, slots), I32),
            v((1, slots), I32),
            v((1, slots), I32),
            v((table_rows, width), BF16),
            v((slots, slots), I32),
            v((slots, feature_dim), BF16),
            v((width, feature_dim), BF16),
            v((feature_dim, width), BF16),
            v((feature_dim, width), BF16),
            v((feature_dim, width), BF16),
            v((n_batch, 1, 128), I32),
            v((2, n_batch, 1, 128), I32),
            v((entries, 128), I32),
            v((n_batch, PAIR_ROWS, width), BF16),
            v((n_batch, PAIR_ROWS, width), BF16),
            v((n_node, slots, width), BF16),
            v((1, slots), I32),
            v((heads, slots, slots), F32),
            v((slots, width), BF16),
            v((heads, slots, slots), F32),
            v((heads, slots, slots), F32),
            v((heads * 128, 128), F32),
            v((8, 128), F32),
            v((chunks, 2, n_x, quarter, width), BF16),
            v((n_node, slots, width), BF16),
            v((chunks, n_x, quarter, width), BF16),
            v((chunks, n_x, quarter, width), BF16),
            v((chunks, 2, quarter // 2, width), BF16),
            v((chunks, 2, quarter, width), BF16),
            v((chunks, n_z, piece, width), BF16),
            v((chunks, n_z, piece, width), BF16),
            v((n_node, slots, width), BF16),
            v((2, n_batch, PAIR_ROWS, half), BF16),
            v((n_batch, PAIR_ROWS, half), BF16),
            v((2, n_batch, PAIR_ROWS, half), BF16),
            v((8, 128), F32),
            v((n_x, 8, 128), F32),
            v((n_z, 8, 128), F32),
            v((2, table_rows, entries), BF16),
            v((entries, slots), BF16),
            v((chunks, 2, n_x, n_z, piece, width), BF16),
            v((table_rows, half), F32),
            v((8, 128), F32),
            dma((11,)),
            dma((4,)),
            dma((4,)),
            dma((7, chunks)),
            dma((7, chunks)),
            dma((5, chunks)),
            dma((3,)),
            dma((3,)),
            dma((3,)),
            dma((3,)),
            dma((chunks + 2,)),
        ],
        compiler_params=pltpu.CompilerParams(
            collective_id=0, has_side_effects=True, vmem_limit_bytes=61 * 2**20
        ),
        name="layer_and_exchanges",
    )(
        spd_bias.T,
        degree_bias.T,
        lengths.reshape(1, 1),
        owner_shard.reshape(1, slots),
        local_row,
        degree_bucket,
        embed_table,
        spd_bucket.reshape(slots, slots),
        cotangent.reshape(slots, feature_dim),
        w_out,
        w_query,
        w_key,
        w_value,
    )

    square = shaped((feature_dim, width), F32)
    table_grad, query_grad, key_grad, value_grad, out_grad, spd_grad, degree_grad = pl.pallas_call(
        finish_kernel,
        out_shape=(
            shaped((table_rows, half), F32),
            square,
            square,
            square,
            shaped((width, feature_dim), F32),
            shaped((heads, NSPD), F32),
            shaped((heads, NDEG), F32),
        ),
        in_specs=[hbm] * 3,
        out_specs=(hbm,) * 5 + (vmem, vmem),
        scratch_shapes=[
            v((chunks, feature_dim, width), BF16),
            v((8, 128), F32),
            v((table_rows, half), F32),
            v((3, feature_dim, width), F32),
            v((width, feature_dim), F32),
            dma((chunks + 2,)),
            dma((chunks + 1,)),
        ],
        compiler_params=pltpu.CompilerParams(vmem_limit_bytes=61 * 2**20),
        name="write_outputs",
    )(sums.reshape(chunks, feature_dim, width), table_grad, small)
    return table_grad, query_grad, key_grad, value_grad, out_grad, spd_grad.T, degree_grad.T


def solution(mesh):
    placed = (
        P("batch", None),
        P(("batch", "replica"), None, None),
        P(("batch", "replica"), None),
        P(("batch", "replica")),
        P(("batch", "replica"), None, None),
        P(("batch", "replica"), None),
        P(None, "node"),
        P(None, "node"),
        P(None, "node"),
        P("node", None),
        P(None, "node"),
        P(None, "node"),
        P(("batch", "replica"), None, None),
    )
    return jax.shard_map(
        on_device,
        mesh=mesh,
        in_specs=placed,
        out_specs=(
            P("batch", ("node", "replica")),
            P(None, "node"),
            P(None, "node"),
            P(None, "node"),
            P("node", None),
            P(None, "node"),
            P(None, "node"),
        ),
        check_vma=False,
    )
```

```python
import functools

import jax
import jax.numpy as jnp
from jax import lax
from jax.experimental import pallas as pl
from jax.experimental.pallas import tpu as pltpu
from jax.sharding import PartitionSpec as P

HEAD_DIM = 64
NSPD = 16
NDEG = 32
EPS = 1e-05
PAIR_ROWS = 16
Z_SIZE = 8
MESH = pl.DeviceIdType.MESH
F32 = jnp.float32
BF16 = jnp.bfloat16
I32 = jnp.int32


def iota(shape, dim):
    return lax.broadcasted_iota(I32, shape, dim)


def dot(a, b, ca=1, cb=0, precision=None):
    return lax.dot_general(
        a, b, (((ca,), (cb,)), ((), ())), preferred_element_type=F32, precision=precision
    )


def remote(src, dst, send_sem, recv_sem, **where):
    return pltpu.make_async_remote_copy(
        src_ref=src,
        dst_ref=dst,
        send_sem=send_sem,
        recv_sem=recv_sem,
        device_id=where,
        device_id_type=MESH,
    )


def wait_bytes(ref, sem):
    pltpu.make_async_copy(ref, ref, sem).wait()


def train_kernel(
    n_batch,
    n_node,
    spd_bias_ref,
    deg_bias_ref,
    length_hbm,
    owner_hbm,
    local_hbm,
    deg_hbm,
    table_hbm,
    spd_hbm,
    cot_hbm,
    wo_hbm,
    wq_hbm,
    wk_hbm,
    wv_hbm,
    out_hbm,
    table_hbm_out,
    small_hbm,
    length_ref,
    owner_v,
    local_v,
    deg_v,
    table_v,
    spd_v,
    cot_v,
    wo_v,
    wq_v,
    wk_v,
    wv_v,
    ask,
    reqs,
    spread,
    rows_send,
    rows_recv,
    rows,
    dest_v,
    bias,
    d_att_v,
    probs_v,
    d_scores,
    sums,
    small,
    grads,
    d_rows_v,
    core_in,
    core_sum,
    x_far_in,
    x_in,
    x_sum,
    z_in,
    y_in,
    pack,
    to_core,
    table_in,
    small_core,
    small_x,
    small_z,
    scatter,
    lists,
    out_ref,
    table_ref,
    small_out,
    lsem,
    gs,
    gr,
    ssem,
    rsem,
    xsem,
    fs,
    fr,
    ts,
    tr,
    wsem,
):
    me_b, me_n, me_r = lax.axis_index("batch"), lax.axis_index("node"), lax.axis_index("replica")
    n_z = Z_SIZE
    n_x = n_batch // n_z
    me_x, me_z = me_b // n_z, me_b % n_z
    other = 1 - me_r
    up, down, across_x = lax.rem(me_x + 1, n_x), lax.rem(me_x + 3, n_x), lax.rem(me_x + 2, n_x)
    slots, feature_dim = cot_v.shape
    table_rows, width = table_v.shape
    heads = width // HEAD_DIM
    blocks = feature_dim // width
    half = width // 2
    entries = n_batch * PAIR_ROWS
    chunks = out_ref.shape[0]
    piece = out_ref.shape[4]
    quarter = n_z * piece
    copies = 2.0 * n_batch
    scale = HEAD_DIM ** (-0.5)
    step = 32
    z_order = (4, 3, 5, 2, 6, 1, 7)
    barrier = pltpu.get_barrier_semaphore()

    def signal_batch(j, carry):
        p = lax.rem(me_b + j, n_batch)
        pl.semaphore_signal(barrier, inc=1, device_id={"batch": p}, device_id_type=MESH)
        return carry

    lax.fori_loop(1, n_batch, signal_batch, 0)
    for j in range(1, n_node):
        p = lax.rem(me_n + j, n_node)
        pl.semaphore_signal(barrier, inc=1, device_id={"node": p}, device_id_type=MESH)
    pl.semaphore_signal(barrier, inc=1, device_id={"replica": other}, device_id_type=MESH)

    columns = pl.ds(pl.multiple_of(me_n * width, width), width)
    loads = [
        pltpu.make_async_copy(src, dst, lsem.at[i])
        for i, (src, dst) in enumerate(
            (
                (owner_hbm, owner_v),
                (local_hbm, local_v),
                (deg_hbm, deg_v),
                (spd_hbm, spd_v),
                (table_hbm.at[:, columns], table_v),
                (cot_hbm, cot_v),
                (wo_hbm, wo_v),
                (wq_hbm, wq_v),
                (wk_hbm, wk_v),
                (wv_hbm, wv_v),
                (length_hbm, length_ref),
            )
        )
    ]
    for load in loads:
        load.start()

    loads[0].wait()
    loads[1].wait()
    owner_row = owner_v[...]
    across = jnp.broadcast_to(owner_row, (slots, slots))
    owner_down = jnp.transpose(across)
    same = across == owner_down
    r0, r1 = iota((slots, slots), 0), iota((slots, slots), 1)
    rank_row = jnp.sum(jnp.where(same & (r0 < r1), 1.0, 0.0), axis=0, keepdims=True).astype(I32)
    rank_col = jnp.sum(jnp.where(same & (r1 < r0), 1.0, 0.0), axis=1, keepdims=True).astype(I32)
    dest_v[...] = owner_row * PAIR_ROWS + rank_row
    dest_col = owner_down[:, 0:1] * PAIR_ROWS + rank_col

    wanted = local_v[...] + 1
    hit = owner_row == iota((n_batch, slots), 0)
    high = jnp.where(hit, (wanted // 32).astype(F32), 0.0).astype(BF16)
    low = jnp.where(hit, (wanted % 32).astype(F32), 0.0).astype(BF16)
    at_rank = jnp.where(rank_col == iota((slots, 128), 1), 1.0, 0.0).astype(BF16)
    listed = (dot(high, at_rank) * 32.0 + dot(low, at_rank)).astype(I32)
    for o in range(n_batch):
        ask[o] = listed[o : o + 1, :]

    pl.semaphore_wait(barrier, n_batch - 1 + n_node - 1 + 1)

    def send_ask(j, carry):
        p = lax.rem(me_b + j, n_batch)
        remote(ask.at[p], reqs.at[me_r, me_b], gs.at[0], gr.at[0], batch=p).start()
        return carry

    lax.fori_loop(1, n_batch, send_ask, 0)
    reqs[me_r, me_b] = ask[me_b]

    loads[2].wait()
    loads[3].wait()

    def bias_block(i, carry):
        at = pl.ds(pl.multiple_of(i * step, step), step)
        bucket = spd_v[at, :]
        terms = [jnp.full(bucket.shape, spd_bias_ref[h, 0], F32) for h in range(heads)]
        for b in range(1, NSPD):
            is_b = bucket == b
            terms = [jnp.where(is_b, spd_bias_ref[h, b], terms[h]) for h in range(heads)]
        for h in range(heads):
            bias[h, at, :] = terms[h]
        return carry

    lax.fori_loop(0, slots // step, bias_block, 0)
    place = jnp.where(iota((slots, entries), 1) == dest_col, 1.0, 0.0).astype(BF16)

    loads[4].wait()
    wait_bytes(ask.at[pl.ds(0, n_batch - 1)], gr.at[0])
    remote(reqs.at[me_r], reqs.at[me_r], gs.at[1], gr.at[1], replica=other).start()
    group = n_z * PAIR_ROWS
    mine = iota((group, 128), 1) == iota((group, 128), 0) % PAIR_ROWS
    for dx in (2, 1, 3, 0):
        first = lax.rem(me_x + dx, n_x) * n_z
        for k in range(n_z):
            spread[k * PAIR_ROWS : (k + 1) * PAIR_ROWS, :] = jnp.broadcast_to(
                reqs[me_r, first + k], (PAIR_ROWS, 128)
            )
        listed = spread[0:group, :].astype(F32)
        target = jnp.sum(jnp.where(mine, listed, 0.0), axis=1, keepdims=True).astype(I32) - 1
        pick = jnp.where(iota((group, table_rows), 1) == target, 1.0, 0.0).astype(BF16)
        rows_send[pl.ds(first, n_z)] = (
            dot(pick, table_v[...]).astype(BF16).reshape(n_z, PAIR_ROWS, width)
        )
        for dz in z_order + ((0,) if dx else ()):
            p = first + lax.rem(me_z + dz, n_z)
            remote(rows_send.at[p], rows_recv.at[me_b], gs.at[2], gr.at[2], batch=p).start()
    rows_recv[me_b] = rows_send[me_b]

    loads[5].wait()
    loads[6].wait()
    loads[10].wait()
    length = length_ref[...]
    d_masked = jnp.where(
        iota((slots, feature_dim), 0) < length, cot_v[...].astype(F32), 0.0
    ).astype(BF16)
    cot_v[...] = d_masked
    d_att_v[...] = dot(d_masked, wo_v[...], 1, 1).astype(BF16)
    degree = deg_v[...]
    deg_terms = []
    for h in range(heads):
        term = jnp.full(degree.shape, deg_bias_ref[h, 0], F32)
        for b in range(1, NDEG):
            term = jnp.where(degree == b, deg_bias_ref[h, b], term)
        deg_terms.append(term)

    wait_bytes(rows_recv.at[pl.ds(0, n_batch - 1)], gr.at[2])
    rows[me_n] = dot(place, rows_recv[...].reshape(entries, width)).astype(BF16)
    for j in (2, 1, 3):
        p = lax.rem(me_n + j, n_node)
        remote(rows.at[me_n], rows.at[me_n], gs.at[3], gr.at[3], node=p).start()
    wait_bytes(reqs.at[0], gr.at[1])
    mine = iota((entries, 128), 1) == iota((entries, 128), 0) % PAIR_ROWS
    targets = []
    for r in range(2):
        for p in range(n_batch):
            spread[p * PAIR_ROWS : (p + 1) * PAIR_ROWS, :] = jnp.broadcast_to(
                reqs[r, p], (PAIR_ROWS, 128)
            )
        target = jnp.sum(jnp.where(mine, spread[...].astype(F32), 0.0), axis=1, keepdims=True) - 1.0
        flat = jnp.transpose(jnp.broadcast_to(target, (entries, 128)))[0:1, :].astype(I32)
        targets.append(flat)
    row = iota((table_rows, entries), 0)
    for r in range(2):
        scatter[r] = jnp.where(row == targets[r], 1.0, 0.0).astype(BF16)
    lists[...] = jnp.where(iota((entries, slots), 0) == dest_v[...], 1.0, 0.0).astype(BF16)
    for load in loads[7:10]:
        load.wait()
    wait_bytes(rows.at[pl.ds(0, n_node - 1)], gr.at[3])

    def core_send(c):
        remote(grads.at[c, other], core_in.at[c], ssem.at[0, c], rsem.at[0, c], replica=other).start()

    first_half, last_half = pl.ds(0, quarter // 2), pl.ds(quarter // 2, quarter // 2)

    straight = (0, 1)

    def x_far(c):
        wait_bytes(core_in.at[c], rsem.at[0, c])
        core_sum[c] = (grads[c, me_r].astype(F32) + core_in[c].astype(F32)).astype(BF16)
        for d, (to, part) in enumerate(((up, first_half), (down, last_half))):
            remote(
                core_sum.at[c, across_x, part],
                x_far_in.at[c, d],
                ssem.at[1, c],
                rsem.at[1, c],
                batch=(across_x if c in straight else to) * n_z + me_z,
            ).start()

    def x_share(c, d, to, part):
        remote(
            core_sum.at[c, to, part],
            x_in.at[c, d, part],
            ssem.at[6, c],
            rsem.at[6, c],
            batch=to * n_z + me_z,
        ).start()

    def x_own(c):
        x_share(c, 0, up, last_half)
        x_share(c, 1, down, first_half)
        if c in straight:
            x_share(c, 0, up, first_half)
            x_share(c, 1, down, last_half)

    def x_near(c):
        if c in straight:
            return
        wait_bytes(x_far_in.at[c], rsem.at[1, c])
        for d, (to, part) in enumerate(((up, first_half), (down, last_half))):
            core_sum[c, to, part] = (
                core_sum[c, to, part].astype(F32) + x_far_in[c, d].astype(F32)
            ).astype(BF16)
            x_share(c, d, to, part)

    def z_send(c):
        wait_bytes(x_in.at[c], rsem.at[6, c])
        total = core_sum[c, me_x].astype(F32) + x_in[c, 0].astype(F32) + x_in[c, 1].astype(F32)
        if c in straight:
            wait_bytes(x_far_in.at[c], rsem.at[1, c])
            total = total + x_far_in[c].astype(F32).reshape(quarter, width)
        x_sum[c] = total.astype(BF16).reshape(n_z, piece, width)
        for j in z_order:
            p = lax.rem(me_z + j, n_z)
            remote(
                x_sum.at[c, p],
                z_in.at[c, me_z],
                ssem.at[2, c],
                rsem.at[2, c],
                batch=me_x * n_z + p,
            ).start()
        z_in[c, me_z] = x_sum[c, me_z]

    def z_back(c):
        wait_bytes(z_in.at[c, pl.ds(0, n_z - 1)], rsem.at[2, c])
        total = z_in[c, 0].astype(F32)
        for z in range(1, n_z):
            total = total + z_in[c, z].astype(F32)
        out_ref[c, me_r, me_x, me_z] = (total * (1.0 / copies)).astype(BF16)
        done = out_ref.at[c, me_r, me_x, me_z]
        for j in z_order:
            p = lax.rem(me_z + j, n_z)
            remote(done, done, ssem.at[3, c], rsem.at[3, c], batch=me_x * n_z + p).start()

    def core_back(c, x):
        done = out_ref.at[c, me_r, x]
        remote(done, done, ssem.at[5, c], rsem.at[5, c], replica=other).start()

    low, high = pl.ds(0, n_z // 2), pl.ds(n_z // 2, n_z // 2)

    def x_give(c, k, source, part, to):
        done = out_ref.at[c, me_r, source, part]
        remote(done, done, ssem.at[4, c], xsem.at[k, c], batch=to * n_z + me_z).start()

    def x_back(c):
        wait_bytes(out_ref.at[c, 0, 0, pl.ds(0, n_z - 1)], rsem.at[3, c])
        x_give(c, 0, me_x, low, up)
        x_give(c, 1, me_x, high, down)
        x_give(c, 2, me_x, high, up)
        x_give(c, 3, me_x, low, down)
        if c == chunks - 1:
            x_give(c, 4, me_x, pl.ds(0, n_z), across_x)

    def x_pass(c):
        wait_bytes(out_ref.at[c, 0, 0, low], xsem.at[0, c])
        if c < chunks - 1:
            x_give(c, 4, down, low, up)
        wait_bytes(out_ref.at[c, 0, 0, low], xsem.at[1, c])
        if c < chunks - 1:
            x_give(c, 4, up, high, down)

    def x_done(c):
        wait_bytes(out_ref.at[c, 0, 0, low], xsem.at[2, c])
        core_back(c, down)
        wait_bytes(out_ref.at[c, 0, 0, low], xsem.at[3, c])
        core_back(c, up)

    def x_last(c):
        wait_bytes(out_ref.at[c, 0, 0], xsem.at[4, c])
        core_back(c, across_x)

    x = jnp.concatenate([rows[b] for b in range(blocks)], axis=1).astype(F32)
    centred = x - jnp.mean(x, axis=1, keepdims=True)
    inv_std = lax.rsqrt(jnp.mean(centred * centred, axis=1, keepdims=True) + EPS)
    x_hat = centred * inv_std
    normed = x_hat.astype(BF16)
    queries = dot(normed, wq_v[...]).astype(BF16)
    keys = dot(normed, wk_v[...]).astype(BF16)
    values = dot(normed, wv_v[...]).astype(BF16)
    normed_t = jnp.transpose(normed)
    d_att = d_att_v[...]

    lane_head = iota((slots, width), 1) // HEAD_DIM

    def only(h, a):
        return jnp.where(lane_head == h, a, jnp.zeros_like(a))

    valid = iota((slots, slots), 1) < length
    attended = jnp.zeros((slots, width), F32)
    d_values = jnp.zeros((slots, width), F32)
    for h in range(heads):
        scores = dot(only(h, queries), keys, 1, 1) * scale + bias[h] + deg_terms[h]
        scores = jnp.where(valid, scores, -jnp.inf)
        exps = jnp.exp(scores - jnp.max(scores, axis=1, keepdims=True))
        probs = exps / jnp.sum(exps, axis=1, keepdims=True)
        probs_v[h] = probs
        probs_b = probs.astype(BF16)
        attended = attended + dot(probs_b, only(h, values))
        d_values = d_values + dot(probs_b, only(h, d_att), 0, 0)
    out_part = dot(attended.astype(BF16), cot_v[...], 0, 0).astype(BF16)
    for b in range(blocks):
        for k in range(2):
            grads[0, b // 2, 2 * (b % 2) + k] = out_part[
                k * quarter : (k + 1) * quarter, b * width : (b + 1) * width
            ]
    core_send(0)
    halves = (2, n_x, quarter, width)
    d_values = d_values.astype(BF16)
    grads[1] = dot(normed_t, d_values).astype(BF16).reshape(halves)
    core_send(1)

    d_queries = jnp.zeros((slots, width), F32)
    d_keys = jnp.zeros((slots, width), F32)
    for h in range(heads):
        probs = probs_v[h]
        d_probs = dot(only(h, d_att), values, 1, 1)
        ds = probs * (d_probs - jnp.sum(probs * d_probs, axis=1, keepdims=True))
        d_scores[h] = ds
        ds_b = ds.astype(BF16)
        d_queries = d_queries + dot(ds_b, only(h, keys))
        d_keys = d_keys + dot(ds_b, only(h, queries), 0, 0)
    d_queries = (d_queries * scale).astype(BF16)
    d_keys = (d_keys * scale).astype(BF16)
    x_far(0)
    x_far(1)
    grads[2] = dot(normed_t, d_keys).astype(BF16).reshape(halves)
    core_send(2)
    grads[3] = dot(normed_t, d_queries).astype(BF16).reshape(halves)
    core_send(3)

    d_normed = (
        dot(d_queries, wq_v[...], 1, 1)
        + dot(d_keys, wk_v[...], 1, 1)
        + dot(d_values, wv_v[...], 1, 1)
    )
    lead = jnp.where(me_n == 0, 1.0, 0.0)
    d_rows = lead * cot_v[...].astype(F32) + inv_std * (
        d_normed
        - jnp.mean(d_normed, axis=1, keepdims=True)
        - x_hat * jnp.mean(d_normed * x_hat, axis=1, keepdims=True)
    )
    for b in range(blocks):
        d_rows_v[b] = d_rows[:, b * width : (b + 1) * width].astype(BF16)
    for j in (2, 1, 3):
        p = lax.rem(me_n + j, n_node)
        remote(d_rows_v.at[p], y_in.at[me_n], fs.at[0], fr.at[0], node=p).start()
    y_in[me_n] = d_rows_v[me_n]

    def bucket_sums(h):
        def spd_block(i, totals):
            at = pl.ds(pl.multiple_of(i * step, step), step)
            bucket, ds = spd_v[at, :], d_scores[h, at, :]
            new = []
            for b in range(NSPD):
                kept = jnp.where(bucket == b, ds, 0.0)
                kept = kept[:, :128] + kept[:, 128:]
                new.append(totals[b] + (kept[0:8] + kept[8:16]) + (kept[16:24] + kept[24:32]))
            return tuple(new)

        totals = lax.fori_loop(
            0, slots // step, spd_block, tuple(jnp.zeros((8, 128), F32) for _ in range(NSPD))
        )
        sums[h * 128 : (h + 1) * 128, :] = jnp.zeros((128, 128), F32)
        for b in range(NSPD):
            at = h * 128 + b
            sums[at : at + 1, :] = jnp.sum(totals[b], axis=0, keepdims=True)
        by_key = jnp.sum(d_scores[h], axis=0, keepdims=True)
        kept = jnp.where(degree == iota((NDEG, slots), 0), by_key, 0.0)
        at = h * 128 + NSPD
        sums[at : at + NDEG, :] = kept[:, :128] + kept[:, 128:]

    x_far(2)
    x_far(3)
    for c in range(chunks):
        x_own(c)
    bucket_sums(0)
    for c in range(chunks):
        x_near(c)
    bucket_sums(1)
    for c in range(chunks):
        z_send(c)

    wait_bytes(y_in.at[pl.ds(0, n_node - 1)], fr.at[0])
    d_rows = y_in[0].astype(F32)
    for n in range(1, n_node):
        d_rows = d_rows + y_in[n].astype(F32)
    packed = dot(lists[...], d_rows.astype(BF16)).astype(BF16)
    left, right = packed[:, :half], packed[:, half:]
    shape = (n_batch, PAIR_ROWS, half)
    to_core[...] = jnp.where(me_r == 0, right, left).reshape(shape)
    remote(to_core, pack.at[me_r], fs.at[1], fr.at[1], replica=other).start()
    pack[me_r] = jnp.where(me_r == 0, left, right).reshape(shape)

    bucket_sums(2)
    z_back(0)
    z_back(1)
    bucket_sums(3)
    totals = dot(jnp.ones((8, 128), F32), sums[...], 1, 1, precision=lax.Precision.HIGHEST)
    small[...] = jnp.zeros_like(small)
    for h in range(heads):
        small[h : h + 1, :] = totals[0:1, h * 128 : (h + 1) * 128]
    remote(small, small_core, ts.at[0], tr.at[0], replica=other).start()
    z_back(2)
    z_back(3)
    wait_bytes(to_core, fr.at[1])
    for dx in (2, 1, 3, 0):
        first = lax.rem(me_x + dx, n_x) * n_z
        for dz in z_order + ((0,) if dx else ()):
            p = first + lax.rem(me_z + dz, n_z)
            remote(pack.at[:, p], table_in.at[:, me_b], fs.at[2], fr.at[2], batch=p).start()
    table_in[:, me_b] = pack[:, me_b]

    wait_bytes(small_core, tr.at[0])
    small_x[me_x] = small[...] + small_core[...]
    for to in (across_x, up, down):
        remote(
            small_x.at[me_x], small_x.at[me_x], ts.at[1], tr.at[1], batch=to * n_z + me_z
        ).start()

    for c in range(chunks):
        x_back(c)
    for c in range(chunks):
        core_back(c, me_x)
    for c in range(chunks):
        x_pass(c)
    wait_bytes(small_x.at[pl.ds(0, n_x - 1)], tr.at[1])
    total = small_x[0]
    for x in range(1, n_x):
        total = total + small_x[x]
    small_z[me_z] = total
    for j in z_order:
        p = lax.rem(me_z + j, n_z)
        remote(
            small_z.at[me_z], small_z.at[me_z], ts.at[2], tr.at[2], batch=me_x * n_z + p
        ).start()

    for c in range(chunks):
        x_done(c)
    wait_bytes(table_in.at[:, pl.ds(0, n_batch - 1)], fr.at[2])
    table_ref[...] = dot(scatter[0], table_in[0].reshape(entries, half)) + dot(
        scatter[1], table_in[1].reshape(entries, half)
    )
    writes = [pltpu.make_async_copy(table_ref, table_hbm_out, wsem.at[chunks])]
    writes[0].start()
    for c in range(chunks):
        x_last(c)
    wait_bytes(small_z.at[pl.ds(0, n_z - 1)], tr.at[2])
    total = small_z[0]
    for z in range(1, n_z):
        total = total + small_z[z]
    small_out[...] = total * (1.0 / copies)
    writes.append(pltpu.make_async_copy(small_out, small_hbm, wsem.at[chunks + 1]))
    writes[-1].start()
    for c in range(chunks):
        wait_bytes(out_ref.at[c, 0], rsem.at[5, c])
        writes.append(pltpu.make_async_copy(out_ref.at[c], out_hbm.at[c], wsem.at[c]))
        writes[-1].start()

    wait_bytes(ask.at[pl.ds(0, n_batch - 1)], gs.at[0])
    wait_bytes(reqs.at[0], gs.at[1])
    wait_bytes(rows_send.at[pl.ds(0, n_batch - 1)], gs.at[2])
    wait_bytes(rows.at[pl.ds(0, n_node - 1)], gs.at[3])
    wait_bytes(y_in.at[pl.ds(0, n_node - 1)], fs.at[0])
    wait_bytes(to_core, fs.at[1])
    wait_bytes(table_in.at[:, pl.ds(0, n_batch - 1)], fs.at[2])
    wait_bytes(small_core, ts.at[0])
    wait_bytes(small_x.at[pl.ds(0, n_x - 1)], ts.at[1])
    wait_bytes(small_z.at[pl.ds(0, n_z - 1)], ts.at[2])
    for c in range(chunks):
        wait_bytes(core_in.at[c], ssem.at[0, c])
        wait_bytes(x_far_in.at[c], ssem.at[1, c])
        wait_bytes(x_in.at[c], ssem.at[6, c])
        wait_bytes(z_in.at[c, pl.ds(0, n_z - 1)], ssem.at[2, c])
        wait_bytes(out_ref.at[c, 0, 0, pl.ds(0, n_z - 1)], ssem.at[3, c])
        wait_bytes(out_ref.at[c, 0, pl.ds(0, n_x - 1)], ssem.at[4, c])
        wait_bytes(out_ref.at[c, 0], ssem.at[5, c])
    for write in writes:
        write.wait()


def finish_kernel(
    sums_hbm,
    table_hbm,
    small_hbm,
    table_out,
    query_out,
    key_out,
    value_out,
    out_out,
    spd_out,
    deg_out,
    sums_v,
    small_v,
    table_v,
    wide,
    outer,
    rsem,
    wsem,
):
    chunks = sums_v.shape[0]
    width = outer.shape[0]
    reads = [
        pltpu.make_async_copy(sums_hbm.at[c], sums_v.at[c], rsem.at[c]) for c in range(chunks)
    ]
    reads.append(pltpu.make_async_copy(small_hbm, small_v, rsem.at[chunks]))
    reads.append(pltpu.make_async_copy(table_hbm, table_v, rsem.at[chunks + 1]))
    for read in reads:
        read.start()
    reads[0].wait()
    step = 64
    steps = width // step

    def widen_outer(i, carry):
        at = pl.ds(pl.multiple_of(i * step, step), step)
        for b in range(outer.shape[1] // width):
            row = pl.ds(pl.multiple_of(i * step + b * width, step), step)
            outer[at, b * width : (b + 1) * width] = sums_v[0, row].astype(F32)
        return carry

    lax.fori_loop(0, steps, widen_outer, 0)
    writes = [pltpu.make_async_copy(outer, out_out, wsem.at[0])]
    writes[0].start()
    for c, out in ((1, value_out), (2, key_out), (3, query_out)):
        reads[c].wait()

        def widen(i, carry, c=c):
            at = pl.ds(pl.multiple_of(i * width, width), width)
            wide[c - 1, at] = sums_v[c, at].astype(F32)
            return carry

        lax.fori_loop(0, sums_v.shape[1] // width, widen, 0)
        writes.append(pltpu.make_async_copy(wide.at[c - 1], out, wsem.at[c]))
        writes[-1].start()
    reads[chunks + 1].wait()
    writes.append(pltpu.make_async_copy(table_v, table_out, wsem.at[chunks]))
    writes[-1].start()
    reads[chunks].wait()
    heads = spd_out.shape[0]
    spd_out[...] = small_v[0:heads, 0:NSPD]
    deg_out[...] = small_v[0:heads, NSPD : NSPD + NDEG]
    for write in writes:
        write.wait()


def on_device(
    embed_table,
    owner_shard,
    local_row,
    lengths,
    spd_bucket,
    degree_bucket,
    w_query,
    w_key,
    w_value,
    w_out,
    spd_bias,
    degree_bias,
    cotangent,
):
    n_batch, n_node = lax.axis_size("batch"), lax.axis_size("node")
    n_z = Z_SIZE
    n_x = n_batch // n_z
    _, slots, feature_dim = cotangent.shape
    table_rows = embed_table.shape[0]
    width = feature_dim // n_node
    half = width // 2
    heads = width // HEAD_DIM
    entries = n_batch * PAIR_ROWS
    chunks = 4
    quarter = feature_dim // (2 * n_x)
    piece = quarter // n_z
    vmem = pl.BlockSpec(memory_space=pltpu.VMEM)
    smem = pl.BlockSpec(memory_space=pltpu.SMEM)
    hbm = pl.BlockSpec(memory_space=pltpu.HBM)
    shaped = jax.ShapeDtypeStruct
    dma = pltpu.SemaphoreType.DMA
    v = pltpu.VMEM

    sums, table_grad, small = pl.pallas_call(
        functools.partial(train_kernel, n_batch, n_node),
        out_shape=(
            shaped((chunks, 2, n_x, n_z, piece, width), BF16),
            shaped((table_rows, half), F32),
            shaped((8, 128), F32),
        ),
        in_specs=[smem] * 2 + [hbm] * 11,
        out_specs=(hbm, hbm, hbm),
        scratch_shapes=[
            v((1, 1), I32),
            v((1, slots), I32),
            v((1, slots), I32),
            v((1, slots), I32),
            v((table_rows, width), BF16),
            v((slots, slots), I32),
            v((slots, feature_dim), BF16),
            v((width, feature_dim), BF16),
            v((feature_dim, width), BF16),
            v((feature_dim, width), BF16),
            v((feature_dim, width), BF16),
            v((n_batch, 1, 128), I32),
            v((2, n_batch, 1, 128), I32),
            v((entries, 128), I32),
            v((n_batch, PAIR_ROWS, width), BF16),
            v((n_batch, PAIR_ROWS, width), BF16),
            v((n_node, slots, width), BF16),
            v((1, slots), I32),
            v((heads, slots, slots), F32),
            v((slots, width), BF16),
            v((heads, slots, slots), F32),
            v((heads, slots, slots), F32),
            v((heads * 128, 128), F32),
            v((8, 128), F32),
            v((chunks, 2, n_x, quarter, width), BF16),
            v((n_node, slots, width), BF16),
            v((chunks, n_x, quarter, width), BF16),
            v((chunks, n_x, quarter, width), BF16),
            v((chunks, 2, quarter // 2, width), BF16),
            v((chunks, 2, quarter, width), BF16),
            v((chunks, n_z, piece, width), BF16),
            v((chunks, n_z, piece, width), BF16),
            v((n_node, slots, width), BF16),
            v((2, n_batch, PAIR_ROWS, half), BF16),
            v((n_batch, PAIR_ROWS, half), BF16),
            v((2, n_batch, PAIR_ROWS, half), BF16),
            v((8, 128), F32),
            v((n_x, 8, 128), F32),
            v((n_z, 8, 128), F32),
            v((2, table_rows, entries), BF16),
            v((entries, slots), BF16),
            v((chunks, 2, n_x, n_z, piece, width), BF16),
            v((table_rows, half), F32),
            v((8, 128), F32),
            dma((11,)),
            dma((4,)),
            dma((4,)),
            dma((7, chunks)),
            dma((7, chunks)),
            dma((5, chunks)),
            dma((3,)),
            dma((3,)),
            dma((3,)),
            dma((3,)),
            dma((chunks + 2,)),
        ],
        compiler_params=pltpu.CompilerParams(
            collective_id=0, has_side_effects=True, vmem_limit_bytes=61 * 2**20
        ),
        name="layer_and_exchanges",
    )(
        spd_bias.T,
        degree_bias.T,
        lengths.reshape(1, 1),
        owner_shard.reshape(1, slots),
        local_row,
        degree_bucket,
        embed_table,
        spd_bucket.reshape(slots, slots),
        cotangent.reshape(slots, feature_dim),
        w_out,
        w_query,
        w_key,
        w_value,
    )

    square = shaped((feature_dim, width), F32)
    table_grad, query_grad, key_grad, value_grad, out_grad, spd_grad, degree_grad = pl.pallas_call(
        finish_kernel,
        out_shape=(
            shaped((table_rows, half), F32),
            square,
            square,
            square,
            shaped((width, feature_dim), F32),
            shaped((heads, NSPD), F32),
            shaped((heads, NDEG), F32),
        ),
        in_specs=[hbm] * 3,
        out_specs=(hbm,) * 5 + (vmem, vmem),
        scratch_shapes=[
            v((chunks, feature_dim, width), BF16),
            v((8, 128), F32),
            v((table_rows, half), F32),
            v((3, feature_dim, width), F32),
            v((width, feature_dim), F32),
            dma((chunks + 2,)),
            dma((chunks + 1,)),
        ],
        compiler_params=pltpu.CompilerParams(vmem_limit_bytes=61 * 2**20),
        name="write_outputs",
    )(sums.reshape(chunks, feature_dim, width), table_grad, small)
    return table_grad, query_grad, key_grad, value_grad, out_grad, spd_grad.T, degree_grad.T


def solution(mesh):
    placed = (
        P("batch", None),
        P(("batch", "replica"), None, None),
        P(("batch", "replica"), None),
        P(("batch", "replica")),
        P(("batch", "replica"), None, None),
        P(("batch", "replica"), None),
        P(None, "node"),
        P(None, "node"),
        P(None, "node"),
        P("node", None),
        P(None, "node"),
        P(None, "node"),
        P(("batch", "replica"), None, None),
    )
    return jax.shard_map(
        on_device,
        mesh=mesh,
        in_specs=placed,
        out_specs=(
            P("batch", ("node", "replica")),
            P(None, "node"),
            P(None, "node"),
            P(None, "node"),
            P("node", None),
            P(None, "node"),
            P(None, "node"),
        ),
        check_vma=False,
    )
```
